32 devices in a mesh: grp: 2 (over x), dp: 16 (over z, y, core).
Axes of the slice: x: 2, y: 2, z: 4, core: 2. Of those that a mesh axis runs over, the one named last changes fastest.
Arguments:
- tokens: bfloat16 [32768, 768], P(('grp', 'dp')), may hold values from -6 to 6
- cotangent: bfloat16 [32768, 768], P(('grp', 'dp')), may hold values from -6 to 6
- w_query: bfloat16 [768, 768], replicated, may hold values from -0.046875 to 0.046875
- w_key: bfloat16 [768, 768], replicated, may hold values from -0.21875 to 0.21875
- w_value: bfloat16 [768, 768], replicated, may hold values from -0.21875 to 0.21875
- w_attn_out: bfloat16 [768, 768], replicated, may hold values from -0.875 to 0.875
- w_inner: bfloat16 [768, 3072], replicated, may hold values from -0.21875 to 0.21875
- w_outer: bfloat16 [3072, 768], replicated, may hold values from -0.15625 to 0.15625
- gain_attn: float32 [768], replicated, may hold values from 0.1 to 1.9
- gain_ffn: float32 [768], replicated, may hold values from 0.1 to 1.9
- bias_table: float32 [32, 12], replicated, may hold values from -4 to 4
- mem_keys: bfloat16 [128, 1536], replicated, may hold values from -6 to 6
- mem_values: bfloat16 [128, 1536], replicated, may hold values from -6 to 6
- mem_ids: int32 [512, 10], P(('grp', 'dp')), may hold values from 0 to 127, all different within a row
- lengths: int32 [512], P(('grp', 'dp')), may hold values from 8 to 64
- buckets: int32 [64, 64], replicated, may hold values from 0 to 31
Outputs:
- out: bfloat16 [32768, 768], P(('grp', 'dp'))
- grad_tokens: bfloat16 [32768, 768], P(('grp', 'dp'))
- grad_w_query: float32 [768, 768], replicated
- grad_w_key: float32 [768, 768], replicated
- grad_w_value: float32 [768, 768], replicated
- grad_w_attn_out: float32 [768, 768], replicated
- grad_w_inner: float32 [768, 3072], replicated
- grad_w_outer: float32 [3072, 768], replicated
- grad_gain_attn: float32 [768], replicated
- grad_gain_ffn: float32 [768], replicated
- grad_bias_table: float32 [32, 12], replicated
- grad_mem_keys: float32 [128, 1536], replicated
- grad_mem_values: float32 [128, 1536], replicated
The draws below stay inside these ranges and needn't reach their ends.
Inputs may be any that keep to these rules, and one draw needn't show every extreme that they name: `lengths`: rows of a question at or past its length are padding. `mem_ids`: the 10 entries of a question are distinct; every entry is named by some question.
All inputs are finite; a program needn't handle non-finite values.
Results may differ from the reference program's by a relative error of at most 0.013.
The reference program's roundings to bfloat16 on the way count: a program that leaves them out, or rounds other values in their place, can miss the bound.
Values sent between devices are 32-bit elements; how exact they have to be, the bound alone decides.
No kernel may reach another device: no remote copies, remote signals or barrier semaphores. Data moves between devices by JAX's collectives and lax.ppermute only.
A program may use at most 256 MiB of HBM per device.

```python
import math
import jax
import jax.numpy as jnp
from jax import lax

D = 768
H = 12
DH = 64
FF = 3072
BUCKETS = 32
SEQ = 64
TOPK = 10
PREFIX = 2
MEM = 128
QUESTIONS = 512
TOKENS = 32768


def touch_ends(array, rng, least, high):
    extent = array.shape
    index_at = [jax.random.randint(jax.random.fold_in(rng, axis), (), 0, extent[axis]) for axis in range(len(extent))]
    array = array.at[tuple(index_at)].set(least)
    longest = extent.index(max(extent))
    index_at[longest] = (index_at[longest] + 1) % extent[longest]
    return array.at[tuple(index_at)].set(high)


def level_of(key, shape, cuts, low, high):
    level, own = 1.0, jax.random.fold_in(key, 6)
    for dim, blocks in cuts:
        heights = jnp.exp(jax.random.uniform(jax.random.fold_in(own, dim), (blocks,), jnp.float32, low / len(cuts), high / len(cuts)))
        level = level * jnp.repeat(heights, shape[dim] // blocks).reshape([-1 if axis == dim else 1 for axis in range(len(shape))])
    return level


def picks_of(stream_key, rows, amount, top, lift):
    sequence = jax.random.permutation(jax.random.fold_in(stream_key, 1), amount)
    boost = sequence
    for power in range(3):
        boost = boost * boost // amount
    boost = boost * lift // amount
    lots = jax.random.randint(jax.random.fold_in(stream_key, 2), (rows, amount), 0, 4096) + boost
    holders = jax.random.permutation(jax.random.fold_in(stream_key, 3), rows)[jnp.arange(amount) % rows]
    lots = jnp.where(jnp.arange(rows)[:, None] == holders[None, :], 1 << 14, lots)
    score = lots * amount + jnp.arange(amount)
    return lax.top_k(score.astype(jnp.int32), top)[1].astype(jnp.int32)


def centred(rng, extent, scale, bound, cuts=(), held_as=jnp.bfloat16):
    entries = scale * jax.random.normal(rng, extent, jnp.float32)
    if cuts:
        entries = entries * level_of(rng, extent, cuts, -0.22, 0.18)
    return jnp.clip(entries, -bound, bound).astype(held_as)


def setup_inputs(seed: int = 0) -> dict:
    keys = jax.random.split(jax.random.key(seed), 17)
    return {
        "tokens": centred(keys[0], (TOKENS, D), 1.0, 6.0, ((0, 32),)),
        "cotangent": centred(keys[1], (TOKENS, D), 1.0, 6.0, ((0, 32),)),
        "w_query": centred(keys[2], (D, D), (D * 25) ** -0.5, 0.046875),
        "w_key": centred(keys[3], (D, D), D ** -0.5, 0.21875),
        "w_value": centred(keys[4], (D, D), D ** -0.5, 0.21875),
        "w_attn_out": centred(keys[5], (D, D), (D // 16) ** -0.5, 0.875),
        "w_inner": centred(keys[6], (D, FF), D ** -0.5, 0.21875),
        "w_outer": centred(keys[7], (FF, D), (FF // 2) ** -0.5, 0.15625),
        "gain_attn": jnp.clip(1.0 + 0.18 * jax.random.normal(keys[8], (D,), jnp.float32), 0.1, 1.9),
        "gain_ffn": jnp.clip(1.0 + 0.18 * jax.random.normal(keys[9], (D,), jnp.float32), 0.1, 1.9),
        "bias_table": centred(keys[10], (BUCKETS, H), 1.0, 4.0, (), jnp.float32),
        "mem_keys": centred(keys[11], (MEM, PREFIX * D), 1.0, 6.0),
        "mem_values": centred(keys[12], (MEM, PREFIX * D), 1.0, 6.0),
        "mem_ids": picks_of(keys[13], QUESTIONS, MEM, TOPK, 640),
        "lengths": touch_ends(jax.random.randint(keys[14], (QUESTIONS,), 8, SEQ + 1), jax.random.fold_in(keys[14], 1), 8, SEQ).astype(jnp.int32),
        "buckets": touch_ends(jax.random.randint(keys[15], (SEQ, SEQ), 0, BUCKETS), jax.random.fold_in(keys[15], 1), 0, BUCKETS - 1).astype(jnp.int32),
    }


@jax.custom_vjp
def low(v):
    return lax.optimization_barrier(v.astype(jnp.bfloat16)).astype(jnp.float32)

@jax.custom_vjp
def low_back(v):
    return v

def low_keep(v):
    return (low(v), None)

def low_pass(kept, grad):
    return (grad,)

def back_keep(v):
    return (v, None)

def back_low(kept, grad):
    return (low(grad),)
low.defvjp(low_keep, low_pass)
low_back.defvjp(back_keep, back_low)
EPS = 1e-06
HIGH = lax.Precision.HIGHEST

def project(left, right):
    return jnp.matmul(left, right, precision=HIGH)

def rms_norm(values, gain):
    return values * lax.rsqrt(lax.optimization_barrier(jnp.mean(values * values, axis=-1, keepdims=True)) + EPS) * gain

def layer(inputs, w_query, w_key, w_value, w_attn_out, w_inner, w_outer, gain_attn, gain_ffn, bias_table, mem_keys, mem_values, entry_ids, lengths, buckets):
    count = inputs.shape[0]
    extra = TOPK * PREFIX
    span = SEQ + extra
    normed1 = low(rms_norm(inputs, gain_attn))
    query = low_back(low(project(normed1, w_query)))
    key_self = low_back(low(project(normed1, w_key)))
    value_self = low_back(low(project(normed1, w_value)))
    mem_key = mem_keys[entry_ids].reshape(count, extra, D)
    mem_value = mem_values[entry_ids].reshape(count, extra, D)
    key_heads = jnp.concatenate([key_self, mem_key], axis=1).reshape(count, span, H, DH)
    value_heads = jnp.concatenate([value_self, mem_value], axis=1).reshape(count, span, H, DH)
    query_heads = query.reshape(count, SEQ, H, DH)
    scores = jnp.einsum('qihe,qjhe->qhij', query_heads, key_heads, precision=HIGH)
    rel_bias = jnp.transpose(bias_table[buckets], (2, 0, 1))
    rel_bias = jnp.concatenate([rel_bias, jnp.zeros((H, SEQ, extra), jnp.float32)], axis=2)
    scores = low_back(scores + rel_bias[None])
    places = jnp.arange(span, dtype=jnp.int32)
    valid = (places[None, :] < lengths[:, None]) | (places[None, :] >= SEQ)
    masked = jnp.where(valid[:, None, None, :], scores, -1000000000.0)
    top = lax.optimization_barrier(jnp.max(masked, axis=-1, keepdims=True))
    expd = jnp.exp(masked - top)
    probs = low(expd / lax.optimization_barrier(jnp.sum(expd, axis=-1, keepdims=True)))
    attended = jnp.einsum('qhij,qjhe->qihe', probs, value_heads, precision=HIGH).reshape(count, SEQ, D)
    attended = low_back(low(attended))
    hidden = inputs + low_back(project(attended, w_attn_out))
    normed2 = low(rms_norm(hidden, gain_ffn))
    inner = low_back(project(normed2, w_inner))
    act = low(jax.nn.gelu(inner, approximate=True))
    return hidden + low_back(project(act, w_outer))

def reference(tokens, cotangent, w_query, w_key, w_value, w_attn_out, w_inner, w_outer, gain_attn, gain_ffn, bias_table, mem_keys, mem_values, mem_ids, lengths, buckets):
    group_size = math.gcd(QUESTIONS, 64)
    steps_count = QUESTIONS // group_size
    inputs = tokens.astype(jnp.float32).reshape(steps_count, group_size, SEQ, D)
    cotans = cotangent.astype(jnp.float32).reshape(steps_count, group_size, SEQ, D)
    entry_groups = mem_ids.reshape(steps_count, group_size, TOPK)
    length_groups = lengths.reshape(steps_count, group_size)
    params = (w_query.astype(jnp.float32), w_key.astype(jnp.float32), w_value.astype(jnp.float32), w_attn_out.astype(jnp.float32), w_inner.astype(jnp.float32), w_outer.astype(jnp.float32), gain_attn.astype(jnp.float32), gain_ffn.astype(jnp.float32), bias_table.astype(jnp.float32), mem_keys.astype(jnp.float32), mem_values.astype(jnp.float32))

    def step(carry, item):
        block_in, block_cot, block_ids, block_len = item

        def forward(block, *weights):
            return layer(block, *weights, block_ids, block_len, buckets)
        result, pull = jax.vjp(forward, block_in, *params)
        grads = pull(block_cot)
        carry = tuple((a + b for a, b in zip(carry, grads[1:])))
        return (carry, (result.astype(jnp.bfloat16), grads[0].astype(jnp.bfloat16)))
    zeros = tuple((jnp.zeros(p.shape, jnp.float32) for p in params))
    totals, (outputs, grad_in) = lax.scan(step, zeros, (inputs, cotans, entry_groups, length_groups))
    out = outputs.reshape(TOKENS, D)
    grad_tokens = grad_in.reshape(TOKENS, D)
    return (out, grad_tokens, totals[0], totals[1], totals[2], totals[3], totals[4], totals[5], totals[6], totals[7], totals[8], totals[9], totals[10])
```

```python
import functools

import jax
import jax.numpy as jnp
from jax import lax
from jax.experimental import pallas as pl
from jax.experimental.pallas import tpu as pltpu
from jax.sharding import PartitionSpec as P

EPS = 1e-06
NEG = -1000000000.0
F32 = jnp.float32
BF16 = jnp.bfloat16
GELU_C = 0.7978845608028654
GELU_A = 0.044715
SMALL = 64
VMEM_LIMIT = 60 * 1024 * 1024
VMEM = pl.BlockSpec(memory_space=pltpu.VMEM)
SMEM = pl.BlockSpec(memory_space=pltpu.SMEM)
ANY = pl.BlockSpec(memory_space=pl.ANY)
COST = pl.CostEstimate(flops=1, bytes_accessed=1, transcendentals=0)


def nn(left, right):
    return lax.dot_general(left, right, (((1,), (0,)), ((), ())), preferred_element_type=F32)


def nt(left, right):
    return lax.dot_general(left, right, (((1,), (1,)), ((), ())), preferred_element_type=F32)


def tn(left, right):
    return lax.dot_general(left, right, (((0,), (0,)), ((), ())), preferred_element_type=F32)


def params():
    return pltpu.CompilerParams(vmem_limit_bytes=VMEM_LIMIT)


def shape(dims, dtype):
    return jax.ShapeDtypeStruct(dims, dtype)


class Sizes:
    def __init__(self, rows, width, questions, heads, buckets, entries, top, mem_width):
        self.rows = rows
        self.width = width
        self.questions = questions
        self.heads = heads
        self.buckets = buckets
        self.entries = entries
        self.top = top
        self.prefix = mem_width // width
        self.seq = rows // questions
        self.dh = width // heads
        self.pad = -(-top // 16) * 16
        self.span = self.seq + self.prefix * self.pad
        self.quad = 4
        self.qw = self.quad * self.dh
        self.quads = heads // self.quad


def head_mask(sz):
    n = sz.quad * sz.seq
    head = lax.broadcasted_iota(jnp.int32, (n, sz.qw), 0) // sz.seq
    lane = lax.broadcasted_iota(jnp.int32, (n, sz.qw), 1) // sz.dh
    return jnp.where(head == lane, 1.0, 0.0).astype(BF16)


def spread(block, mask, sz):
    return jnp.concatenate([block] * sz.quad, axis=0) * mask


def gather_diag(full, sz):
    s = sz.seq
    lane = lax.broadcasted_iota(jnp.int32, (s, 2 * sz.dh), 1)
    parts = []
    for pair in range(sz.quad // 2):
        cols = slice(pair * 2 * sz.dh, (pair + 1) * 2 * sz.dh)
        low = full[(2 * pair) * s : (2 * pair + 1) * s, cols]
        high = full[(2 * pair + 1) * s : (2 * pair + 2) * s, cols]
        parts.append(jnp.where(lane < sz.dh, low, high))
    return jnp.concatenate(parts, axis=1)


def bucket_lanes(buckets_ref, sz):
    row = lax.broadcasted_iota(jnp.int32, (sz.seq, 2 * sz.seq), 0)
    lane = lax.broadcasted_iota(jnp.int32, (sz.seq, 2 * sz.seq), 1)
    pick = jnp.where(lane % sz.seq == row, 1.0, 0.0).astype(BF16)
    return tn(buckets_ref[...].astype(F32).astype(BF16), pick)


def fill_bias(bias_ref, table_ref, buckets_ref, sz):
    bt = bucket_lanes(buckets_ref, sz)
    width = sz.heads * sz.seq
    head = lax.broadcasted_iota(jnp.int32, (sz.heads, width), 0)
    lane = lax.broadcasted_iota(jnp.int32, (sz.heads, width), 1) // sz.seq
    wide = jnp.dot(
        table_ref[...], jnp.where(head == lane, 1.0, 0.0),
        precision=lax.Precision.HIGHEST, preferred_element_type=F32,
    )
    for pair in range(sz.heads // 2):
        cols = slice(pair * 2 * sz.seq, (pair + 1) * 2 * sz.seq)
        acc = jnp.zeros((sz.seq, 2 * sz.seq), F32)
        for b in range(sz.buckets):
            acc = jnp.where(bt == float(b), wide[b : b + 1, cols], acc)
        bias_ref[0 : sz.seq, cols] = acc
    n = sz.prefix * sz.pad
    row = lax.broadcasted_iota(jnp.int32, (n, sz.heads * sz.seq), 0) % sz.pad
    bias_ref[sz.seq :, :] = jnp.where(row < sz.top, 0.0, NEG)


def fill_memory(pick, table_ref, out_ref):
    out_ref[...] = nn(pick, table_ref[...]).astype(BF16)


def one_hot(ids_ref, sz):
    n = sz.questions * sz.pad
    row = lax.broadcasted_iota(jnp.int32, (n, sz.questions), 0) // sz.pad
    question = lax.broadcasted_iota(jnp.int32, (n, sz.questions), 1)
    repeat = jnp.where(row == question, 1.0, 0.0).astype(BF16)
    spread_ids = nn(repeat, (ids_ref[...] + 1).astype(F32).astype(BF16))
    slot = lax.broadcasted_iota(jnp.int32, (n, sz.top), 0) % sz.pad
    own = slot == lax.broadcasted_iota(jnp.int32, (n, sz.top), 1)
    column = jnp.sum(jnp.where(own, spread_ids, 0.0), axis=1, keepdims=True)
    lane = lax.broadcasted_iota(jnp.int32, (n, sz.entries), 1).astype(F32)
    return jnp.where(lane + 1.0 == column, 1.0, 0.0).astype(BF16)


def key_block(self_ref, mem_ref, q, col, sz):
    rows = pl.ds(pl.multiple_of(q * sz.seq, sz.seq), sz.seq)
    mrows = pl.ds(pl.multiple_of(q * sz.pad, sz.pad), sz.pad)
    parts = [self_ref[rows, col : col + sz.qw]]
    for p in range(sz.prefix):
        parts.append(mem_ref[mrows, p * sz.width + col : p * sz.width + col + sz.qw])
    return jnp.concatenate(parts, axis=0)


def probabilities(keys, spread_query, bias, length, sz):
    scores = nt(keys, spread_query) + bias
    row = lax.broadcasted_iota(jnp.int32, scores.shape, 0)
    admitted = jnp.logical_or(row < length, row >= sz.seq)
    scores = jnp.where(admitted, scores, NEG)
    top = jnp.max(scores, axis=0, keepdims=True)
    expd = jnp.exp(scores - top)
    return expd * (1.0 / jnp.sum(expd, axis=0, keepdims=True))


def forward_kernel(
    sz,
    tokens, wq, wk, wv, wo, gain1, gain2, table, mkeys, mvalues, ids, lengths, buckets,
    normed1, query, key, value, attended, hidden, normed2,
    bias, memk, memv,
):
    block = 256
    pick = one_hot(ids, sz)
    fill_memory(pick, mkeys, memk)
    fill_memory(pick, mvalues, memv)
    fill_bias(bias, table, buckets, sz)
    for r in range(0, sz.rows, block):
        x = tokens[r : r + block, :].astype(F32)
        scale = lax.rsqrt(jnp.mean(x * x, axis=-1, keepdims=True) + EPS)
        low = (x * scale * gain1[...].reshape(1, -1)).astype(BF16)
        normed1[r : r + block, :] = low
    for w, out in ((wq, query), (wk, key), (wv, value)):
        for r in range(0, sz.rows, block):
            out[r : r + block, :] = nn(normed1[r : r + block, :], w[...]).astype(BF16)
    mask = head_mask(sz)

    def step(q, carry):
        length = lengths[q]
        rows = pl.ds(pl.multiple_of(q * sz.seq, sz.seq), sz.seq)
        for c in range(sz.quads):
            col = c * sz.qw
            sq = spread(query[rows, col : col + sz.qw], mask, sz)
            keys = key_block(key, memk, q, col, sz)
            values = key_block(value, memv, q, col, sz)
            probs = probabilities(keys, sq, bias[:, col : col + sz.qw], length, sz)
            full = tn(probs.astype(BF16), values)
            attended[rows, col : col + sz.qw] = gather_diag(full, sz).astype(BF16)
        return carry

    lax.fori_loop(0, sz.questions, step, 0)
    for r in range(0, sz.rows, block):
        rows = slice(r, r + block)
        h = tokens[rows, :].astype(F32) + nn(attended[rows, :], wo[...])
        hidden[rows, :] = h
        scale = lax.rsqrt(jnp.mean(h * h, axis=-1, keepdims=True) + EPS)
        normed2[rows, :] = (h * scale * gain2[...].reshape(1, -1)).astype(BF16)


def forward(sz, tokens, wq, wk, wv, wo, gain1, gain2, table, mkeys, mvalues, ids, lengths, buckets):
    n, d = sz.rows, sz.width
    low = shape((n, d), BF16)
    return pl.pallas_call(
        functools.partial(forward_kernel, sz),
        in_specs=[VMEM] * 11 + [SMEM, VMEM],
        out_specs=[VMEM] * 7,
        out_shape=[low, low, low, low, low, shape((n, d), F32), low],
        scratch_shapes=[
            pltpu.VMEM((sz.span, sz.heads * sz.seq), F32),
            pltpu.VMEM((sz.questions * sz.pad, sz.prefix * d), BF16),
            pltpu.VMEM((sz.questions * sz.pad, sz.prefix * d), BF16),
        ],
        compiler_params=params(),
        cost_estimate=COST,
        name="forward",
    )(tokens, wq, wk, wv, wo, gain1, gain2, table, mkeys, mvalues, ids, lengths, buckets)


def ffn_kernel(core, normed2, cot, wi, wo, act, d_inner, keep, send):
    block = 256
    n = normed2.shape[0]
    for r in range(0, n, block):
        rows = slice(r, r + block)
        v = nn(normed2[rows, :], wi[...])
        d_act = nt(cot[rows, :], wo[...])
        sq = v * v
        t = jnp.tanh(v * (GELU_C + (GELU_C * GELU_A) * sq))
        half = 0.5 + 0.5 * t
        act[rows, :] = (v * half).astype(BF16)
        slope = half + (0.5 * v) * (1.0 - t * t) * (GELU_C + (3.0 * GELU_C * GELU_A) * sq)
        d_inner[rows, :] = (d_act * slope).astype(BF16)

    @pl.when(core[0] == 0)
    def _():
        send[0] = tn(normed2[...], d_inner[...])
        keep[0] = tn(act[...], cot[...])

    @pl.when(core[0] != 0)
    def _():
        send[0] = tn(act[...], cot[...])
        keep[0] = tn(normed2[...], d_inner[...])


def ffn(core, normed2, cot, wi, wo, first, count):
    n, d = normed2.shape
    full = pl.BlockSpec((n, d), lambda j, c: (0, 0))
    cols = pl.BlockSpec((n, d), lambda j, c: (0, j))
    part = pl.BlockSpec((1, d, d), lambda j, c: (j, 0, 0))
    return pl.pallas_call(
        ffn_kernel,
        grid_spec=pltpu.PrefetchScalarGridSpec(
            num_scalar_prefetch=1,
            grid=(count,),
            in_specs=[
                full,
                full,
                pl.BlockSpec((d, d), lambda j, c: (0, first + j)),
                pl.BlockSpec((d, d), lambda j, c: (first + j, 0)),
            ],
            out_specs=[cols, cols, part, part],
        ),
        out_shape=[
            shape((n, count * d), BF16),
            shape((n, count * d), BF16),
            shape((count, d, d), F32),
            shape((count, d, d), F32),
        ],
        compiler_params=params(),
        cost_estimate=COST,
        name="ffn",
    )(core, normed2, cot, wi, wo)


def mid_kernel(
    steps, per, d_in0, d_in1, wi, hidden, cot, gain2, attended, wo,
    d_hidden, d_attended, grad_out, grad_gain, total,
):
    j = pl.program_id(0)
    block = 256
    n = hidden.shape[0]

    @pl.when(j == 0)
    def _():
        total[...] = nt(d_in0[...], wi[...])

    @pl.when(jnp.logical_and(j > 0, j < per))
    def _():
        total[...] += nt(d_in0[...], wi[...])

    @pl.when(j >= per)
    def _():
        total[...] += nt(d_in1[...], wi[...])

    @pl.when(j == steps - 1)
    def _():
        acc = jnp.zeros((1, hidden.shape[1]), F32)
        for r in range(0, n, block):
            rows = slice(r, r + block)
            h = hidden[rows, :]
            scale = lax.rsqrt(jnp.mean(h * h, axis=-1, keepdims=True) + EPS)
            base = h * scale
            d_normed = total[rows, :]
            scaled = d_normed * gain2[...].reshape(1, -1)
            acc = acc + jnp.sum(d_normed * base, axis=0, keepdims=True)
            back = scale * (scaled - base * jnp.mean(scaled * base, axis=-1, keepdims=True))
            d_h = cot[rows, :].astype(F32) + back
            d_hidden[rows, :] = d_h
            total[rows, :] = d_h
            d_attended[rows, :] = nt(d_h.astype(BF16), wo[...]).astype(BF16)
        grad_gain[...] = acc
        grad_out[...] = tn(attended[...], total[...].astype(BF16))


def mid(d_in0, d_in1, wi, hidden, cot, gain2, attended, wo):
    n, d = hidden.shape
    per = d_in0.shape[1] // d
    steps = 2 * per
    full = pl.BlockSpec((n, d), lambda j: (0, 0))
    square = pl.BlockSpec((d, d), lambda j: (0, 0))
    row = pl.BlockSpec((1, d), lambda j: (0, 0))
    gain = pl.BlockSpec((d,), lambda j: (0,))
    return pl.pallas_call(
        functools.partial(mid_kernel, steps, per),
        grid=(steps,),
        in_specs=[
            pl.BlockSpec((n, d), lambda j: (0, jnp.minimum(j, per - 1))),
            pl.BlockSpec((n, d), lambda j: (0, jnp.maximum(j - per, 0))),
            pl.BlockSpec((d, d), lambda j: (0, j)),
            full,
            full,
            gain,
            full,
            square,
        ],
        out_specs=[full, full, square, row],
        out_shape=[shape((n, d), F32), shape((n, d), BF16), shape((d, d), F32), shape((1, d), F32)],
        scratch_shapes=[pltpu.VMEM((n, d), F32)],
        compiler_params=params(),
        cost_estimate=COST,
        name="mid",
    )(d_in0, d_in1, wi, hidden, cot, gain2, attended, wo)


def back_kernel(
    sz,
    core, query, key, value, d_att, normed1, grad_out, mkeys, mvalues, ids, lengths, buckets, table,
    wq, wk, wv, gain1, grad_gain2,
    d_query, d_key, d_value, keep0, send0, keep1, send1,
    bias, memk, memv, d_memk, d_memv, d_bias, sums,
):
    d = sz.width
    pick = one_hot(ids, sz)
    fill_memory(pick, mkeys, memk)
    fill_memory(pick, mvalues, memv)
    fill_bias(bias, table, buckets, sz)
    d_bias[...] = jnp.zeros_like(d_bias)
    mask = head_mask(sz)

    def step(q, carry):
        length = lengths[q]
        rows = pl.ds(pl.multiple_of(q * sz.seq, sz.seq), sz.seq)
        mrows = pl.ds(pl.multiple_of(q * sz.pad, sz.pad), sz.pad)
        for c in range(sz.quads):
            col = c * sz.qw
            cols = slice(col, col + sz.qw)
            sq = spread(query[rows, cols], mask, sz)
            so = spread(d_att[rows, cols], mask, sz)
            keys = key_block(key, memk, q, col, sz)
            values = key_block(value, memv, q, col, sz)
            probs = probabilities(keys, sq, bias[:, cols], length, sz)
            d_probs = nt(values, so)
            d_val = nn(probs.astype(BF16), so)
            inner = jnp.sum(probs * d_probs, axis=0, keepdims=True)
            d_scores = (probs * (d_probs - inner)).astype(BF16)
            d_bias[:, cols] += d_scores[0 : sz.seq, :].astype(F32)
            d_query[rows, cols] = gather_diag(tn(d_scores, keys), sz).astype(BF16)
            d_ky = nn(d_scores, sq)
            d_key[rows, cols] = d_ky[0 : sz.seq, :].astype(BF16)
            d_value[rows, cols] = d_val[0 : sz.seq, :].astype(BF16)
            for p in range(sz.prefix):
                part = slice(sz.seq + p * sz.pad, sz.seq + (p + 1) * sz.pad)
                to = slice(p * d + col, p * d + col + sz.qw)
                d_memk[mrows, to] = d_ky[part, :]
                d_memv[mrows, to] = d_val[part, :]
        return carry

    lax.fori_loop(0, sz.questions, step, 0)

    def table_grad(full):
        high = full[...].astype(BF16)
        rest = (full[...] - high.astype(F32)).astype(BF16)
        return tn(pick, high) + tn(pick, rest)

    def emit(out, left, right, mem):
        out[0:d, :] = tn(left[...], right[...])
        grads = table_grad(mem)
        for p in range(sz.prefix):
            out[d + p * sz.entries : d + (p + 1) * sz.entries, :] = grads[:, p * d : (p + 1) * d]

    bt = bucket_lanes(buckets, sz)
    for pair in range(sz.heads // 2):
        cols = slice(pair * 2 * sz.seq, (pair + 1) * 2 * sz.seq)
        part = d_bias[:, cols]
        for b in range(sz.buckets):
            sums[b : b + 1, cols] = jnp.sum(jnp.where(bt == float(b), part, 0.0), axis=0, keepdims=True)
    width = sz.heads * sz.seq
    flat = sz.heads * sz.buckets
    head_in = lax.broadcasted_iota(jnp.int32, (width, d), 0) // sz.seq
    head_out = lax.broadcasted_iota(jnp.int32, (width, d), 1) // sz.buckets
    by_head = jnp.dot(
        sums[...], jnp.where(head_in == head_out, 1.0, 0.0),
        precision=lax.Precision.HIGHEST, preferred_element_type=F32,
    )
    own = lax.broadcasted_iota(jnp.int32, (sz.buckets, d), 0)
    lane = lax.broadcasted_iota(jnp.int32, (sz.buckets, d), 1)
    here = jnp.logical_and(lane % sz.buckets == own, lane < flat)
    bias_row = jnp.sum(jnp.where(here, by_head, 0.0), axis=0, keepdims=True)

    def small_rows(out, q_ref, k_ref, v_ref):
        terms = wq[...].astype(F32) * q_ref[0:d, :] + wk[...].astype(F32) * k_ref[0:d, :]
        terms = terms + wv[...].astype(F32) * v_ref[0:d, :]
        high = terms.astype(BF16)
        rest = (terms - high.astype(F32)).astype(BF16)
        ones = jnp.ones((8, d), BF16)
        total = (nt(ones, high) + nt(ones, rest))[0:1, :]
        out[d : d + SMALL, :] = jnp.zeros((SMALL, d), F32)
        out[d : d + 1, :] = total / gain1[...].reshape(1, -1)
        out[d + 1 : d + 2, :] = grad_gain2[...]
        out[d + 2 : d + 3, :] = bias_row

    @pl.when(core[0] == 0)
    def _():
        emit(send0, normed1, d_key, d_memv)
        emit(keep0, normed1, d_query, d_memk)
        send1[0:d, :] = grad_out[...]
        send1[d:, :] = jnp.zeros((SMALL, d), F32)
        keep1[0:d, :] = tn(normed1[...], d_value[...])
        small_rows(keep1, keep0, send0, keep1)

    @pl.when(core[0] != 0)
    def _():
        emit(send0, normed1, d_query, d_memk)
        emit(keep0, normed1, d_key, d_memv)
        send1[0:d, :] = tn(normed1[...], d_value[...])
        small_rows(send1, send0, keep0, send1)
        keep1[0:d, :] = grad_out[...]
        keep1[d:, :] = jnp.zeros((SMALL, d), F32)


def back(sz, core, query, key, value, d_att, normed1, grad_out, mkeys, mvalues, ids, lengths, buckets, table,
         wq, wk, wv, gain1, grad_gain2):
    n, d = sz.rows, sz.width
    low = shape((n, d), BF16)
    extra = sz.prefix * sz.entries
    mem = (sz.questions * sz.pad, sz.prefix * d)
    return pl.pallas_call(
        functools.partial(back_kernel, sz),
        in_specs=[SMEM] + [VMEM] * 9 + [SMEM] + [VMEM] * 7,
        out_specs=[VMEM] * 7,
        out_shape=[
            low,
            low,
            low,
            shape((d + extra, d), F32),
            shape((d + extra, d), F32),
            shape((d + SMALL, d), F32),
            shape((d + SMALL, d), F32),
        ],
        scratch_shapes=[
            pltpu.VMEM((sz.span, sz.heads * sz.seq), F32),
            pltpu.VMEM(mem, BF16),
            pltpu.VMEM(mem, BF16),
            pltpu.VMEM(mem, F32),
            pltpu.VMEM(mem, F32),
            pltpu.VMEM((sz.seq, sz.heads * sz.seq), F32),
            pltpu.VMEM((sz.buckets, sz.heads * sz.seq), F32),
        ],
        compiler_params=params(),
        cost_estimate=COST,
        name="back",
    )(core, query, key, value, d_att, normed1, grad_out, mkeys, mvalues, ids, lengths, buckets, table,
      wq, wk, wv, gain1, grad_gain2)


def last_kernel(tokens, d_hidden, gain1, d_query, d_key, d_value, wq, wk, wv, grad_tokens):
    block = 256
    for r in range(0, tokens.shape[0], block):
        rows = slice(r, r + block)
        d_normed = nt(d_query[rows, :], wq[...])
        d_normed = d_normed + nt(d_key[rows, :], wk[...])
        d_normed = d_normed + nt(d_value[rows, :], wv[...])
        x = tokens[rows, :].astype(F32)
        scale = lax.rsqrt(jnp.mean(x * x, axis=-1, keepdims=True) + EPS)
        base = x * scale
        scaled = d_normed * gain1[...].reshape(1, -1)
        back_in = scale * (scaled - base * jnp.mean(scaled * base, axis=-1, keepdims=True))
        grad_tokens[rows, :] = (d_hidden[rows, :] + back_in).astype(BF16)


def last(tokens, d_hidden, gain1, d_query, d_key, d_value, wq, wk, wv):
    n, d = tokens.shape
    return pl.pallas_call(
        last_kernel,
        in_specs=[VMEM] * 9,
        out_specs=VMEM,
        out_shape=shape((n, d), BF16),
        compiler_params=params(),
        cost_estimate=COST,
        name="last",
    )(tokens, d_hidden, gain1, d_query, d_key, d_value, wq, wk, wv)


def output_kernel(steps, per, hidden, act0, act1, wo, out, total):
    j = pl.program_id(0)

    @pl.when(j == 0)
    def _():
        total[...] = hidden[...] + nn(act0[...], wo[...])

    @pl.when(jnp.logical_and(j > 0, j < per))
    def _():
        total[...] += nn(act0[...], wo[...])

    @pl.when(jnp.logical_and(j >= per, j < steps - 1))
    def _():
        total[...] += nn(act1[...], wo[...])

    @pl.when(j == steps - 1)
    def _():
        out[...] = (total[...] + nn(act1[...], wo[...])).astype(BF16)


def output(hidden, act0, act1, wo):
    n, d = hidden.shape
    per = act0.shape[1] // d
    steps = 2 * per
    full = pl.BlockSpec((n, d), lambda j: (0, 0))
    return pl.pallas_call(
        functools.partial(output_kernel, steps, per),
        grid=(steps,),
        in_specs=[
            full,
            pl.BlockSpec((n, d), lambda j: (0, jnp.minimum(j, per - 1))),
            pl.BlockSpec((n, d), lambda j: (0, jnp.maximum(j - per, 0))),
            pl.BlockSpec((d, d), lambda j: (j, 0)),
        ],
        out_specs=full,
        out_shape=shape((n, d), BF16),
        scratch_shapes=[pltpu.VMEM((n, d), F32)],
        compiler_params=params(),
        cost_estimate=COST,
        name="output",
    )(hidden, act0, act1, wo)


CORE = ("dp", 1)
LINK_Y = ("dp", 2)
LINK_X = ("grp", 1)


def swap(value, link, sizes):
    axis, stride = link
    return lax.ppermute(value, axis, [(i, i ^ stride) for i in range(sizes[axis])])


def bit_of(link):
    axis, stride = link
    return (lax.axis_index(axis) // stride) % 2


def add_split_kernel(bits, *refs):
    count = len(refs) // 6
    for i in range(count):
        k0, r0, k1, r1 = refs[4 * i : 4 * i + 4]
        keep, send = refs[4 * count + 2 * i : 4 * count + 2 * i + 2]
        send[...] = k1[...].reshape(send.shape) + r1[...].reshape(send.shape)
        keep[...] = k0[...].reshape(keep.shape) + r0[...].reshape(keep.shape)


def add_split(bits, parts):
    steps = 2
    in_specs, out_specs, outs, operands = [], [], [], []
    for i, (kept, got, lead) in enumerate(parts):
        rows, d = kept.shape[-2:]
        rb = rows // 2 // steps
        for mine in (True, False):
            def index(j, b, i=i, mine=mine, lead=lead):
                half = b[i] if mine else 1 - b[i]
                place = (half * steps + j, 0)
                return place if lead is None else (lead,) + place

            spec = pl.BlockSpec((rb, d) if lead is None else (1, rb, d), index)
            in_specs += [spec, spec]
            operands += [kept, got]
            out_specs.append(pl.BlockSpec((rb, d), lambda j, b: (j, 0)))
            outs.append(shape((rows // 2, d), F32))
    total = sum(o.shape[0] * o.shape[1] for o in outs)
    result = pl.pallas_call(
        add_split_kernel,
        grid_spec=pltpu.PrefetchScalarGridSpec(
            num_scalar_prefetch=1, grid=(steps,), in_specs=in_specs, out_specs=out_specs
        ),
        out_shape=outs,
        compiler_params=params(),
        cost_estimate=COST,
        name="add_split",
    )(bits, *operands)
    return [(result[2 * i], result[2 * i + 1]) for i in range(len(parts))]


def add_pairs_kernel(a, b, c, d, out0, out1):
    out0[...] = a[...] + b[...]
    out1[...] = c[...] + d[...]


def add_pairs(a, b, c, d):
    return pl.pallas_call(
        add_pairs_kernel,
        in_specs=[VMEM] * 4,
        out_specs=[VMEM] * 2,
        out_shape=[shape(a.shape, F32), shape(c.shape, F32)],
        compiler_params=params(),
        cost_estimate=COST,
        name="add_pairs",
    )(a, b, c, d)


def join_kernel(bits, a, b, c, d, out0, out1):
    for first, own, got, out in ((0, a, b, out0), (1, c, d, out1)):
        n = own.shape[0]
        out[pl.ds(pl.multiple_of(bits[first] * n, 8), n), :] = own[...]
        out[pl.ds(pl.multiple_of((1 - bits[first]) * n, 8), n), :] = got[...]


def join(bits, a, b, c, d):
    return pl.pallas_call(
        join_kernel,
        in_specs=[SMEM] + [VMEM] * 4,
        out_specs=[VMEM] * 2,
        out_shape=[shape((2 * a.shape[0], a.shape[1]), F32), shape((2 * c.shape[0], c.shape[1]), F32)],
        compiler_params=params(),
        cost_estimate=COST,
        name="join",
    )(bits, a, b, c, d)


def rest_groups(size, low):
    return [[i for i in range(size) if i % low == r] for r in range(low)]


class Order:
    def __init__(self):
        self.done = None

    def after(self, value):
        if self.done is not None:
            value, _ = lax.optimization_barrier((value, self.done))
        return value

    def run(self, kernel, first, *rest):
        result = kernel(self.after(first), *rest)
        self.done = jax.tree.leaves(result)[0]
        return result


class Reduction:
    def __init__(self, order, sizes, turn_by, keep, send):
        self.order = order
        self.sizes = sizes
        self.turn_by = turn_by
        x_bit, y_bit = bit_of(LINK_X), bit_of(LINK_Y)
        self.xy = jnp.stack([x_bit, y_bit]).astype(jnp.int32)
        self.yx = jnp.stack([y_bit, x_bit]).astype(jnp.int32)
        self.place_bits = jnp.stack([bit_of(CORE), x_bit, y_bit]).astype(jnp.int32)
        self.kept = keep
        self.send = send

    def begin(self):
        moved = {}
        for array, _ in self.send:
            if id(array) not in moved:
                moved[id(array)] = swap(self.order.after(array), CORE, self.sizes)
        self.got = [(moved[id(array)], lead) for array, lead in self.send]

    def first(self):
        parts = [(k, g, lead) for (k, lead), (g, _) in zip(self.kept, self.got)]
        (self.k0, s0), (self.k1, s1) = self.order.run(add_split, self.xy, parts)
        self.r0, self.r1 = swap(s0, LINK_X, self.sizes), swap(s1, LINK_Y, self.sizes)

    def second(self):
        parts = [(self.k0, self.r0, None), (self.k1, self.r1, None)]
        (self.k0, s0), (self.k1, s1) = self.order.run(add_split, self.yx, parts)
        self.r0, self.r1 = swap(s0, LINK_Y, self.sizes), swap(s1, LINK_X, self.sizes)

    def third(self):
        pair = tuple(self.order.run(add_pairs, self.k0, self.r0, self.k1, self.r1))
        groups = rest_groups(self.sizes["dp"], 4)
        groups = groups[self.turn_by :] + groups[: self.turn_by]
        pair = lax.psum(pair, "dp", axis_index_groups=groups)
        if self.sizes["grp"] > 2:
            pair = lax.psum(pair, "grp", axis_index_groups=rest_groups(self.sizes["grp"], 2))
        self.pair = pair
        self.r0, self.r1 = swap(pair[0], LINK_Y, self.sizes), swap(pair[1], LINK_X, self.sizes)

    def fourth(self):
        g0, g1 = self.order.run(join, self.yx, self.pair[0], self.r0, self.pair[1], self.r1)
        h0, h1 = swap(g0, LINK_X, self.sizes), swap(g1, LINK_Y, self.sizes)
        self.own = (g0, h0, g1, h1)
        self.other = tuple(swap(v, CORE, self.sizes) for v in self.own)

    def finish(self, plan, outs, olds=()):
        olds = self.order.run(lambda bits: place(0, plan, bits, self.own, outs, olds), self.place_bits)
        return self.order.run(lambda bits: place(1, plan, bits, self.other, outs, olds), self.place_bits)


def place_kernel(other_core, plan, n_out, n_alias, bits, *refs):
    parts = refs[:4]
    outs = refs[4 + n_alias : 4 + n_alias + n_out]
    bufs = refs[4 + n_alias + n_out : 8 + n_alias + n_out]
    in_sems, out_sems = refs[-2:]
    loads = [pltpu.make_async_copy(parts[i], bufs[i], in_sems.at[i]) for i in range(4)]
    for load in loads:
        load.start()
    for load in loads:
        load.wait()
    for core in (0, 1):
        for x_bit in (0, 1):
            for y_bit in (0, 1):
                test = (bits[0] == core) & (bits[1] == x_bit) & (bits[2] == y_bit)

                @pl.when(test)
                def _(core=core, x_bit=x_bit, y_bit=y_bit):
                    copies = []
                    for index in range(4):
                        part, other_half = index // 2, index % 2
                        key = (part, core ^ other_core, (x_bit, y_bit)[part] ^ other_half)
                        for row, rows, out, where in plan[key]:
                            copies.append(
                                pltpu.make_async_copy(
                                    bufs[index].at[pl.ds(row, rows)],
                                    outs[out].at[where],
                                    out_sems.at[len(copies)],
                                )
                            )
                    for copy in copies:
                        copy.start()
                    for copy in copies:
                        copy.wait()


def place(other_core, plan, bits, arrays, outs, olds=()):
    n_copies = sum(len(v) for v in plan.values())
    return pl.pallas_call(
        functools.partial(place_kernel, other_core, plan, len(outs), len(olds)),
        in_specs=[SMEM] + [ANY] * (4 + len(olds)),
        out_specs=[ANY] * len(outs),
        out_shape=outs,
        input_output_aliases={5 + i: i for i in range(len(olds))},
        scratch_shapes=[pltpu.VMEM(a.shape, F32) for a in arrays]
        + [pltpu.SemaphoreType.DMA((4,)), pltpu.SemaphoreType.DMA((n_copies,))],
        compiler_params=params(),
        cost_estimate=COST,
        name="place",
    )(bits, *arrays, *olds)


def ffn_plan(first, d):
    plan = {}
    h = d // 2
    for part in (0, 1):
        at = (first + part) * d
        for half in (0, 1):
            plan[(part, 0, half)] = [(0, h, 0, (pl.ds(at + half * h, h), pl.ds(0, d)))]
            plan[(part, 1, half)] = [(0, h, 1, (pl.ds(half * h, h), pl.ds(at, d)))]
    return plan


def attn_plan(d, entries, prefix):
    plan = {}
    whole = pl.ds(0, d)
    for core, weight, mem in ((0, 0, 4), (1, 1, 5)):
        rows = d + prefix * entries
        h = rows // 2
        blocks = [(0, d, weight, 0)] + [(d + p * entries, entries, mem, p) for p in range(prefix)]
        for half in (0, 1):
            todo = []
            for start, count, out, p in blocks:
                low, high = max(start, half * h), min(start + count, (half + 1) * h)
                if low < high:
                    where = (pl.ds(low - start, high - low), pl.ds(p * d, d) if out >= 4 else whole)
                    todo.append((low - half * h, high - low, out, where))
            plan[(0, core, half)] = todo
    for core, blocks in ((0, [(0, d, 2), (d, SMALL, 6)]), (1, [(0, d, 3)])):
        h = (d + SMALL) // 2
        for half in (0, 1):
            todo = []
            for start, count, out in blocks:
                low, high = max(start, half * h), min(start + count, (half + 1) * h)
                if low < high:
                    todo.append((low - half * h, high - low, out, (pl.ds(low - start, high - low), whole)))
            plan[(1, core, half)] = todo
    return plan


def body(
    sizes,
    tokens,
    cotangent,
    w_query,
    w_key,
    w_value,
    w_attn_out,
    w_inner,
    w_outer,
    gain_attn,
    gain_ffn,
    bias_table,
    mem_keys,
    mem_values,
    mem_ids,
    lengths,
    buckets,
):
    questions, top = mem_ids.shape
    n, d = tokens.shape
    sz = Sizes(n, d, questions, bias_table.shape[1], bias_table.shape[0], mem_keys.shape[0], top, mem_keys.shape[1])
    core = bit_of(CORE).reshape(1).astype(jnp.int32)
    order = Order()
    half = w_inner.shape[1] // d // 2
    ffn_outs = [shape(w_outer.shape, F32), shape(w_inner.shape, F32)]
    square = shape((d, d), F32)
    mem = shape(mem_keys.shape, F32)

    normed1, query, key, value, attended, hidden, normed2 = order.run(
        functools.partial(forward, sz), tokens, w_query, w_key, w_value, w_attn_out, gain_attn, gain_ffn, bias_table,
        mem_keys, mem_values, mem_ids, lengths, buckets,
    )
    act0, d_in0, keep_a, send_a = order.run(ffn, core, normed2, cotangent, w_inner, w_outer, 0, half)
    red_a = Reduction(order, sizes, 0, [(keep_a, 0), (keep_a, 1)], [(send_a, 0), (send_a, 1)])
    red_a.begin()
    act1, d_in1, keep_b, send_b = order.run(ffn, core, normed2, cotangent, w_inner, w_outer, half, half)
    red_b = Reduction(order, sizes, 1, [(keep_b, 0), (keep_b, 1)], [(send_b, 0), (send_b, 1)])
    red_b.begin()
    red_a.first()
    d_hidden, d_attended, grad_out, grad_gain2 = order.run(
        mid, d_in0, d_in1, w_inner, hidden, cotangent, gain_ffn, attended, w_attn_out
    )
    red_b.first()
    red_a.second()
    d_query, d_key, d_value, keep0, send0, keep1, send1 = order.run(
        functools.partial(back, sz),
        core, query, key, value, d_attended, normed1, grad_out, mem_keys, mem_values,
        mem_ids, lengths, buckets, bias_table, w_query, w_key, w_value, gain_attn, grad_gain2,
    )
    red_c = Reduction(order, sizes, 2, [(keep0, None), (keep1, None)], [(send0, None), (send1, None)])
    red_a.third()
    red_c.begin()
    red_b.second()
    red_c.first()
    grad_tokens = order.run(
        last, tokens, d_hidden, gain_attn, d_query, d_key, d_value, w_query, w_key, w_value
    )
    red_b.third()
    red_a.fourth()
    out = order.run(output, hidden, act0, act1, w_outer)
    red_c.second()
    red_c.third()
    red_b.fourth()
    grads = red_a.finish(ffn_plan(0, d), ffn_outs)
    grad_w_outer, grad_w_inner = red_b.finish(ffn_plan(half, d), ffn_outs, grads)
    red_c.fourth()
    gq, gk, gv, go, gmk, gmv, small = red_c.finish(
        attn_plan(d, sz.entries, sz.prefix),
        [square, square, square, square, mem, mem, shape((SMALL, d), F32)],
    )
    return (
        out,
        grad_tokens,
        gq,
        gk,
        gv,
        go,
        grad_w_inner,
        grad_w_outer,
        small[0],
        small[1],
        small[2, : sz.heads * sz.buckets].reshape(sz.heads, sz.buckets).T,
        gmk,
        gmv,
    )


def solution(mesh):
    split = P(("grp", "dp"), None)
    placed = (split, split) + (P(),) * 11 + (split, P(("grp", "dp")), P())
    return jax.shard_map(
        functools.partial(body, dict(mesh.shape)),
        mesh=mesh,
        in_specs=placed,
        out_specs=(split, split) + (P(),) * 11,
        check_vma=False,
    )
```

```python
import functools

import jax
import jax.numpy as jnp
from jax import lax
from jax.experimental import pallas as pl
from jax.experimental.pallas import tpu as pltpu
from jax.sharding import PartitionSpec as P

EPS = 1e-06
NEG = -1000000000.0
F32 = jnp.float32
BF16 = jnp.bfloat16
GELU_C = 0.7978845608028654
GELU_A = 0.044715
SMALL = 64
UNIT_ROWS = 512
UNROLL_FORWARD = 8
UNROLL_BACK = 4
VMEM_LIMIT = 64 * 1024 * 1024
VMEM = pl.BlockSpec(memory_space=pltpu.VMEM)
SMEM = pl.BlockSpec(memory_space=pltpu.SMEM)
ANY = pl.BlockSpec(memory_space=pl.ANY)
PLAN = (
    "fwd", "e0", "e1", "w0", "w1", "e2", "A1", "e3", "w2", "mid", "w3", "A2", "B1", "back", "Cb0", "Az0",
    "Cb1", "B2", "C1", "Az1", "out", "Bz0", "Az2", "last", "Bz1", "Az3", "A4", "C2", "A5", "An", "Bz2", "C3",
    "Bz3", "B4", "A6", "Apn", "B5", "Apf", "B6", "AB", "Cc", "C4", "Bn", "C5", "Cm", "Bpf", "Cpn", "Bpn",
    "C6", "Cpf",
)

COSTS = {"A1": 6e+09, "A2": 6e+09, "Ap": 4e+10, "Az1": 6e+09, "B1": 4e+10, "Bz1": 3e+09, "Bz2": 2e+10, "Cz2": 1e+10, "back": 4e+10, "e": 1e+10}


def cost(name):
    return pl.CostEstimate(flops=int(COSTS.get(name, 1)), bytes_accessed=1, transcendentals=0)


def nn(left, right):
    return lax.dot_general(left, right, (((1,), (0,)), ((), ())), preferred_element_type=F32)


def nt(left, right):
    return lax.dot_general(left, right, (((1,), (1,)), ((), ())), preferred_element_type=F32)


def tn(left, right):
    return lax.dot_general(left, right, (((0,), (0,)), ((), ())), preferred_element_type=F32)


class Copies:
    def __init__(self, sems):
        self.sems, self.made = sems, []

    def start(self, source, target):
        copy = pltpu.make_async_copy(source, target, self.sems.at[len(self.made)])
        copy.start()
        self.made.append(copy)
        return copy

    def wait(self):
        for copy in self.made:
            copy.wait()


def params():
    return pltpu.CompilerParams(vmem_limit_bytes=VMEM_LIMIT)


def shape(dims, dtype):
    return jax.ShapeDtypeStruct(dims, dtype)


class Sizes:
    def __init__(self, rows, width, questions, heads, buckets, entries, top, mem_width):
        self.rows = rows
        self.width = width
        self.questions = questions
        self.heads = heads
        self.buckets = buckets
        self.entries = entries
        self.top = top
        self.prefix = mem_width // width
        self.seq = rows // questions
        self.dh = width // heads
        self.pad = -(-top // 16) * 16
        self.span = self.seq + self.prefix * self.pad
        self.quad = 4
        self.qw = self.quad * self.dh
        self.quads = heads // self.quad


def head_mask(sz):
    n = sz.quad * sz.seq
    head = lax.broadcasted_iota(jnp.int32, (n, sz.qw), 0) // sz.seq
    lane = lax.broadcasted_iota(jnp.int32, (n, sz.qw), 1) // sz.dh
    return jnp.where(head == lane, 1.0, 0.0).astype(BF16)


def spread(block, mask, sz):
    return jnp.concatenate([block] * sz.quad, axis=0) * mask


def gather_diag(full, sz):
    s = sz.seq
    lane = lax.broadcasted_iota(jnp.int32, (s, 2 * sz.dh), 1)
    parts = []
    for pair in range(sz.quad // 2):
        cols = slice(pair * 2 * sz.dh, (pair + 1) * 2 * sz.dh)
        low = full[(2 * pair) * s : (2 * pair + 1) * s, cols]
        high = full[(2 * pair + 1) * s : (2 * pair + 2) * s, cols]
        parts.append(jnp.where(lane < sz.dh, low, high))
    return jnp.concatenate(parts, axis=1)


def bucket_lanes(buckets_ref, sz):
    row = lax.broadcasted_iota(jnp.int32, (sz.seq, 2 * sz.seq), 0)
    lane = lax.broadcasted_iota(jnp.int32, (sz.seq, 2 * sz.seq), 1)
    pick = jnp.where(lane % sz.seq == row, 1.0, 0.0).astype(BF16)
    return tn(buckets_ref[...].astype(F32).astype(BF16), pick)


def fill_bias(bias_ref, table_ref, buckets_ref, sz):
    bt = bucket_lanes(buckets_ref, sz)
    width = sz.heads * sz.seq
    head = lax.broadcasted_iota(jnp.int32, (sz.heads, width), 0)
    lane = lax.broadcasted_iota(jnp.int32, (sz.heads, width), 1) // sz.seq
    wide = lax.dot_general(
        table_ref[...], jnp.where(head == lane, 1.0, 0.0), (((0,), (0,)), ((), ())),
        precision=lax.Precision.HIGHEST, preferred_element_type=F32,
    )
    for pair in range(sz.heads // 2):
        cols = slice(pair * 2 * sz.seq, (pair + 1) * 2 * sz.seq)
        acc = jnp.zeros((sz.seq, 2 * sz.seq), F32)
        for b in range(sz.buckets):
            acc = jnp.where(bt == float(b), wide[b : b + 1, cols], acc)
        bias_ref[0 : sz.seq, cols] = acc
    n = sz.prefix * sz.pad
    row = lax.broadcasted_iota(jnp.int32, (n, sz.heads * sz.seq), 0) % sz.pad
    bias_ref[sz.seq :, :] = jnp.where(row < sz.top, 0.0, NEG)


def fill_memory(pick, table_ref, out_ref):
    out_ref[...] = nn(pick, table_ref[...]).astype(BF16)


def one_hot(ids_ref, sz):
    n = sz.questions * sz.pad
    row = lax.broadcasted_iota(jnp.int32, (n, sz.questions), 0) // sz.pad
    question = lax.broadcasted_iota(jnp.int32, (n, sz.questions), 1)
    repeat = jnp.where(row == question, 1.0, 0.0).astype(BF16)
    spread_ids = nn(repeat, (ids_ref[...] + 1).astype(F32).astype(BF16))
    slot = lax.broadcasted_iota(jnp.int32, (n, sz.top), 0) % sz.pad
    own = slot == lax.broadcasted_iota(jnp.int32, (n, sz.top), 1)
    column = jnp.sum(jnp.where(own, spread_ids, 0.0), axis=1, keepdims=True)
    lane = lax.broadcasted_iota(jnp.int32, (n, sz.entries), 1).astype(F32)
    return jnp.where(lane + 1.0 == column, 1.0, 0.0).astype(BF16)


def key_block(self_ref, mem_ref, q, col, sz):
    rows = pl.ds(pl.multiple_of(q * sz.seq, sz.seq), sz.seq)
    mrows = pl.ds(pl.multiple_of(q * sz.pad, sz.pad), sz.pad)
    parts = [self_ref[rows, col : col + sz.qw]]
    for p in range(sz.prefix):
        parts.append(mem_ref[mrows, p * sz.width + col : p * sz.width + col + sz.qw])
    return jnp.concatenate(parts, axis=0)


def probabilities(keys, spread_query, bias, length, sz):
    scores = nt(keys, spread_query) + bias
    row = lax.broadcasted_iota(jnp.int32, scores.shape, 0)
    admitted = jnp.logical_or(row < length, row >= sz.seq)
    scores = jnp.where(admitted, scores, NEG)
    top = jnp.max(scores, axis=0, keepdims=True)
    expd = jnp.exp(scores - top)
    return expd * (1.0 / jnp.sum(expd, axis=0, keepdims=True))


def forward_kernel(
    sz,
    tokens_hbm, wq_hbm, wk_hbm, wv_hbm, wo_hbm, gain1, gain2, table, mkeys, mvalues, ids, lengths, buckets,
    normed1_hbm, query_hbm, key_hbm, value_hbm, attended_hbm, hidden_hbm, normed2_hbm,
    tokens, weights, normed1, query, key, value, attended, hidden, normed2,
    bias, memk, memv, in_sems, out_sems,
):
    block = 256
    loads, stores = Copies(in_sems), Copies(out_sems)
    sources = [tokens_hbm, wq_hbm, wk_hbm, wv_hbm, wo_hbm]
    targets = [tokens] + [weights.at[i] for i in range(4)]
    loaded = [loads.start(a, b) for a, b in zip(sources, targets)]
    pick = one_hot(ids, sz)
    fill_memory(pick, mkeys, memk)
    fill_memory(pick, mvalues, memv)
    fill_bias(bias, table, buckets, sz)
    loaded[0].wait()
    for r in range(0, sz.rows, block):
        x = tokens[r : r + block, :].astype(F32)
        scale = lax.rsqrt(jnp.mean(x * x, axis=-1, keepdims=True) + EPS)
        low = (x * scale * gain1[...].reshape(1, -1)).astype(BF16)
        normed1[r : r + block, :] = low
    stores.start(normed1, normed1_hbm)
    for i, (out, out_hbm) in enumerate(((query, query_hbm), (key, key_hbm), (value, value_hbm))):
        loaded[1 + i].wait()
        for r in range(0, sz.rows, block):
            out[r : r + block, :] = nn(normed1[r : r + block, :], weights[i]).astype(BF16)
        stores.start(out, out_hbm)
    mask = head_mask(sz)

    def step(q, carry):
        length = lengths[q]
        rows = pl.ds(pl.multiple_of(q * sz.seq, sz.seq), sz.seq)
        for c in range(sz.quads):
            col = c * sz.qw
            sq = spread(query[rows, col : col + sz.qw], mask, sz)
            keys = key_block(key, memk, q, col, sz)
            values = key_block(value, memv, q, col, sz)
            probs = probabilities(keys, sq, bias[:, col : col + sz.qw], length, sz)
            full = tn(probs.astype(BF16), values)
            attended[rows, col : col + sz.qw] = gather_diag(full, sz).astype(BF16)
        return carry

    lax.fori_loop(0, sz.questions, step, 0, unroll=UNROLL_FORWARD)
    stores.start(attended, attended_hbm)
    loaded[4].wait()
    for r in range(0, sz.rows, block):
        rows = slice(r, r + block)
        h = tokens[rows, :].astype(F32) + nn(attended[rows, :], weights[3])
        hidden[rows, :] = h
        scale = lax.rsqrt(jnp.mean(h * h, axis=-1, keepdims=True) + EPS)
        normed2[rows, :] = (h * scale * gain2[...].reshape(1, -1)).astype(BF16)
        stores.start(hidden.at[pl.ds(r, block)], hidden_hbm.at[pl.ds(r, block)])
        stores.start(normed2.at[pl.ds(r, block)], normed2_hbm.at[pl.ds(r, block)])
    stores.wait()


def forward(step, sz, tokens, wq, wk, wv, wo, gain1, gain2, table, mkeys, mvalues, ids, lengths, buckets):
    n, d = sz.rows, sz.width
    low = shape((n, d), BF16)
    outs = [low, low, low, low, low, shape((n, d), F32), low]
    mem = (sz.questions * sz.pad, sz.prefix * d)
    return pl.pallas_call(
        functools.partial(forward_kernel, sz),
        in_specs=[ANY] * 5 + [VMEM] * 6 + [SMEM, VMEM],
        out_specs=[ANY] * 7,
        out_shape=outs,
        scratch_shapes=[pltpu.VMEM((n, d), BF16), pltpu.VMEM((4, d, d), BF16)]
        + [pltpu.VMEM(o.shape, o.dtype) for o in outs]
        + [
            pltpu.VMEM((sz.span, sz.heads * sz.seq), F32),
            pltpu.VMEM(mem, BF16),
            pltpu.VMEM(mem, BF16),
            pltpu.SemaphoreType.DMA((5,)),
            pltpu.SemaphoreType.DMA((5 + 2 * (n // 256),)),
        ],
        compiler_params=params(),
        cost_estimate=cost(step),
        name="forward",
    )(tokens, wq, wk, wv, wo, gain1, gain2, table, mkeys, mvalues, ids, lengths, buckets)


def unit_kernel(olds, normed2, cot, wi, wo, *refs):
    act, d_inner = refs[olds:]
    v = nn(normed2[...], wi[...])
    d_act = nt(cot[...], wo[...])
    sq = v * v
    t = jnp.tanh(v * (GELU_C + (GELU_C * GELU_A) * sq))
    half = 0.5 + 0.5 * t
    act[...] = (v * half).astype(BF16)
    slope = half + (0.5 * v) * (1.0 - t * t) * (GELU_C + (3.0 * GELU_C * GELU_A) * sq)
    d_inner[...] = (d_act * slope).astype(BF16)


def units(step, normed2, cot, wi, wo, quarter, olds=()):
    n, d = normed2.shape
    rows = pl.BlockSpec((UNIT_ROWS, d), lambda j: (j, 0))
    cols = pl.BlockSpec((UNIT_ROWS, d), lambda j: (j, quarter))
    wide = shape((n, wi.shape[1]), BF16)
    return pl.pallas_call(
        functools.partial(unit_kernel, len(olds)),
        grid=(n // UNIT_ROWS,),
        in_specs=[
            rows,
            rows,
            pl.BlockSpec((d, d), lambda j: (0, quarter)),
            pl.BlockSpec((d, d), lambda j: (quarter, 0)),
        ]
        + [ANY] * len(olds),
        out_specs=[cols, cols],
        out_shape=[wide, wide],
        input_output_aliases={4 + i: i for i in range(len(olds))},
        compiler_params=params(),
        cost_estimate=cost(step),
        name="units",
    )(normed2, cot, wi, wo, *olds)


def weight_kernel(
    quarter, core, normed2_hbm, cot_hbm, act_hbm, d_inner_hbm, keep_hbm, send0_hbm, send1_hbm,
    normed2, cot, act, d_inner, grads, in_sems, out_sems,
):
    d = normed2.shape[1]
    h = d // 2
    cols = pl.ds(quarter * d, d)
    loads = Copies(in_sems)
    inner = [loads.start(normed2_hbm, normed2), loads.start(d_inner_hbm.at[:, cols], d_inner)]
    outer = [loads.start(act_hbm.at[:, cols], act), loads.start(cot_hbm, cot)]

    def write(pairs):
        stores = Copies(out_sems)
        targets = [send0_hbm, send1_hbm, keep_hbm.at[pl.ds(0, h)], keep_hbm.at[pl.ds(h, h)]]
        for i, (ready, left, right) in enumerate(pairs):
            if i % 2 == 0:
                for copy in ready:
                    copy.wait()
            half = slice(i % 2 * h, i % 2 * h + h)
            grads[i] = tn(left[:, half], right[...])
            stores.start(grads.at[i], targets[i])
        stores.wait()

    @pl.when(core[0] == 0)
    def _():
        write([(inner, normed2, d_inner)] * 2 + [(outer, act, cot)] * 2)

    @pl.when(core[0] != 0)
    def _():
        write([(outer, act, cot)] * 2 + [(inner, normed2, d_inner)] * 2)


def weights(step, core, normed2, cot, act, d_inner, quarter):
    n, d = normed2.shape
    return pl.pallas_call(
        functools.partial(weight_kernel, quarter),
        in_specs=[SMEM] + [ANY] * 4,
        out_specs=[ANY] * 3,
        out_shape=[shape((d, d), F32)] + [shape((d // 2, d), F32)] * 2,
        scratch_shapes=[pltpu.VMEM((n, d), BF16)] * 4
        + [
            pltpu.VMEM((4, d // 2, d), F32),
            pltpu.SemaphoreType.DMA((4,)),
            pltpu.SemaphoreType.DMA((4,)),
        ],
        compiler_params=params(),
        cost_estimate=cost(step),
        name="weights",
    )(core, normed2, cot, act, d_inner)


def mid_kernel(
    steps, d_in, wi, hidden_hbm, cot_hbm, gain2, attended_hbm, wo_hbm,
    d_hidden_hbm, d_attended_hbm, grad_out_hbm, grad_gain,
    total, hidden, cot, attended, wo, d_hidden, d_attended, grad_out, in_sems, out_sems,
):
    j = pl.program_id(0)
    block = 256
    n = hidden.shape[0]
    loads = ((hidden_hbm, hidden), (cot_hbm, cot), (wo_hbm, wo), (attended_hbm, attended))

    def load(i):
        return pltpu.make_async_copy(*loads[i], in_sems.at[i])

    @pl.when(j == 0)
    def _():
        for i in range(4):
            load(i).start()
        total[...] = nt(d_in[...], wi[...])

    @pl.when(j > 0)
    def _():
        total[...] += nt(d_in[...], wi[...])

    @pl.when(j == steps - 1)
    def _():
        stores = Copies(out_sems)
        for i in range(4):
            load(i).wait()
        acc = jnp.zeros((1, hidden.shape[1]), F32)
        for r in range(0, n, block):
            rows = slice(r, r + block)
            h = hidden[rows, :]
            scale = lax.rsqrt(jnp.mean(h * h, axis=-1, keepdims=True) + EPS)
            base = h * scale
            d_normed = total[rows, :]
            scaled = d_normed * gain2[...].reshape(1, -1)
            acc = acc + jnp.sum(d_normed * base, axis=0, keepdims=True)
            back = scale * (scaled - base * jnp.mean(scaled * base, axis=-1, keepdims=True))
            d_h = cot[rows, :].astype(F32) + back
            d_hidden[rows, :] = d_h
            low = d_h.astype(BF16)
            cot[rows, :] = low
            d_attended[rows, :] = nt(low, wo[...]).astype(BF16)
            where = pl.ds(r, block)
            stores.start(d_hidden.at[where], d_hidden_hbm.at[where])
            stores.start(d_attended.at[where], d_attended_hbm.at[where])
        grad_gain[...] = acc
        half = grad_out.shape[0] // 2
        for i in (0, 1):
            grad_out[i * half : (i + 1) * half, :] = tn(attended[:, i * half : (i + 1) * half], cot[...])
            where = pl.ds(i * half, half)
            stores.start(grad_out.at[where], grad_out_hbm.at[where])
        stores.wait()


def mid(step, d_in, wi, hidden, cot, gain2, attended, wo):
    n, d = hidden.shape
    steps = d_in.shape[1] // d
    return pl.pallas_call(
        functools.partial(mid_kernel, steps),
        grid=(steps,),
        in_specs=[
            pl.BlockSpec((n, d), lambda j: (0, j)),
            pl.BlockSpec((d, d), lambda j: (0, j)),
            ANY,
            ANY,
            pl.BlockSpec((d,), lambda j: (0,)),
            ANY,
            ANY,
        ],
        out_specs=[ANY, ANY, ANY, pl.BlockSpec((1, d), lambda j: (0, 0))],
        out_shape=[shape((n, d), F32), shape((n, d), BF16), shape((d, d), F32), shape((1, d), F32)],
        scratch_shapes=[
            pltpu.VMEM((n, d), F32),
            pltpu.VMEM((n, d), F32),
            pltpu.VMEM((n, d), BF16),
            pltpu.VMEM((n, d), BF16),
            pltpu.VMEM((d, d), BF16),
            pltpu.VMEM((n, d), F32),
            pltpu.VMEM((n, d), BF16),
            pltpu.VMEM((d, d), F32),
            pltpu.SemaphoreType.DMA((4,)),
            pltpu.SemaphoreType.DMA((2 * (n // 256) + 2,)),
        ],
        compiler_params=params(),
        cost_estimate=cost(step),
        name="mid",
    )(d_in, wi, hidden, cot, gain2, attended, wo)


def back_kernel(
    sz,
    my_core, query_hbm, key_hbm, value_hbm, d_att_hbm, normed1_hbm, grad_out_hbm, mkeys, mvalues, ids, lengths, buckets,
    table, wq_hbm, wk_hbm, wv_hbm, gain1, grad_gain2,
    d_query_hbm, d_key_hbm, d_value_hbm, keep0_hbm, keep1_hbm, send00_hbm, send01_hbm, send10_hbm, send11_hbm,
    query, key, value, d_att, normed1, weights, d_query, d_key, d_value, shares,
    bias, memk, memv, d_memk, d_memv, d_bias, sums, in_sems, out_sems,
):
    d = sz.width
    second = d + sz.prefix * sz.entries
    loads, stores = Copies(in_sems), Copies(out_sems)
    early = [
        loads.start(a, b)
        for a, b in ((query_hbm, query), (key_hbm, key), (value_hbm, value), (d_att_hbm, d_att))
    ]
    late = [loads.start(normed1_hbm, normed1)]
    late += [loads.start(w, weights.at[i]) for i, w in enumerate((wq_hbm, wk_hbm, wv_hbm))]
    late.append(loads.start(grad_out_hbm, shares.at[1, pl.ds(second, d)]))
    pick = one_hot(ids, sz)
    fill_memory(pick, mkeys, memk)
    fill_memory(pick, mvalues, memv)
    fill_bias(bias, table, buckets, sz)
    d_bias[...] = jnp.zeros_like(d_bias)
    mask = head_mask(sz)
    for copy in early:
        copy.wait()

    def step(q, carry):
        length = lengths[q]
        rows = pl.ds(pl.multiple_of(q * sz.seq, sz.seq), sz.seq)
        mrows = pl.ds(pl.multiple_of(q * sz.pad, sz.pad), sz.pad)
        for c in range(sz.quads):
            col = c * sz.qw
            cols = slice(col, col + sz.qw)
            sq = spread(query[rows, cols], mask, sz)
            so = spread(d_att[rows, cols], mask, sz)
            keys = key_block(key, memk, q, col, sz)
            values = key_block(value, memv, q, col, sz)
            probs = probabilities(keys, sq, bias[:, cols], length, sz)
            d_probs = nt(values, so)
            d_val = nn(probs.astype(BF16), so)
            inner = jnp.sum(probs * d_probs, axis=0, keepdims=True)
            d_scores = (probs * (d_probs - inner)).astype(BF16)
            d_bias[:, cols] += d_scores[0 : sz.seq, :].astype(F32)
            d_query[rows, cols] = gather_diag(tn(d_scores, keys), sz).astype(BF16)
            d_ky = nn(d_scores, sq)
            d_key[rows, cols] = d_ky[0 : sz.seq, :].astype(BF16)
            d_value[rows, cols] = d_val[0 : sz.seq, :].astype(BF16)
            for p in range(sz.prefix):
                part = slice(sz.seq + p * sz.pad, sz.seq + (p + 1) * sz.pad)
                to = slice(p * d + col, p * d + col + sz.qw)
                d_memk[mrows, to] = d_ky[part, :]
                d_memv[mrows, to] = d_val[part, :]
        return carry

    lax.fori_loop(0, sz.questions, step, 0, unroll=UNROLL_BACK)
    for a, b in ((d_query, d_query_hbm), (d_key, d_key_hbm), (d_value, d_value_hbm)):
        stores.start(a, b)
    for copy in late:
        copy.wait()

    mine, other = my_core[0], 1 - my_core[0]

    def store(start, keep, halves):
        stores.start(shares.at[mine, pl.ds(start, keep.shape[0])], keep)
        for half in halves:
            stores.start(shares.at[other, pl.ds(start, half.shape[0])], half)
            start += half.shape[0]

    def table_grad(full):
        high = full[...].astype(BF16)
        rest = (full[...] - high.astype(F32)).astype(BF16)
        return tn(pick, high) + tn(pick, rest)

    def emit(core, right, mem):
        shares[core, 0:d, :] = tn(normed1[...], right[...])
        grads = table_grad(mem)
        for p in range(sz.prefix):
            rows = slice(d + p * sz.entries, d + (p + 1) * sz.entries)
            shares[core, rows, :] = grads[:, p * d : (p + 1) * d]

    emit(0, d_query, d_memk)
    emit(1, d_key, d_memv)
    store(0, keep0_hbm, (send00_hbm, send01_hbm))
    shares[0, second : second + d, :] = tn(normed1[...], d_value[...])

    bt = bucket_lanes(buckets, sz)
    for pair in range(sz.heads // 2):
        cols = slice(pair * 2 * sz.seq, (pair + 1) * 2 * sz.seq)
        part = d_bias[:, cols]
        for b in range(sz.buckets):
            sums[b : b + 1, cols] = jnp.sum(jnp.where(bt == float(b), part, 0.0), axis=0, keepdims=True)
    width = sz.heads * sz.seq
    flat = sz.heads * sz.buckets
    head_in = lax.broadcasted_iota(jnp.int32, (width, flat), 0) // sz.seq
    head_out = lax.broadcasted_iota(jnp.int32, (width, flat), 1) // sz.buckets
    by_head = jnp.dot(
        sums[...], jnp.where(head_in == head_out, 1.0, 0.0),
        precision=lax.Precision.HIGHEST, preferred_element_type=F32,
    )
    own = lax.broadcasted_iota(jnp.int32, (sz.buckets, flat), 0)
    lane = lax.broadcasted_iota(jnp.int32, (sz.buckets, flat), 1)
    bias_row = jnp.sum(jnp.where(lane % sz.buckets == own, by_head, 0.0), axis=0, keepdims=True)

    terms = weights[0].astype(F32) * shares[0, 0:d, :] + weights[1].astype(F32) * shares[1, 0:d, :]
    terms = terms + weights[2].astype(F32) * shares[0, second : second + d, :]
    high = terms.astype(BF16)
    rest = (terms - high.astype(F32)).astype(BF16)
    ones = jnp.ones((8, d), BF16)
    total = (nt(ones, high) + nt(ones, rest))[0:1, :]
    small = second + d
    shares[0, small : small + SMALL, :] = jnp.zeros((SMALL, d), F32)
    shares[1, small : small + SMALL, :] = jnp.zeros((SMALL, d), F32)
    shares[0, small : small + 1, :] = total / gain1[...].reshape(1, -1)
    shares[0, small + 1 : small + 2, :] = grad_gain2[...]
    shares[0, small + 2 : small + 3, 0:flat] = bias_row
    store(second, keep1_hbm, (send10_hbm, send11_hbm))
    stores.wait()


def back(step, sz, core, query, key, value, d_att, normed1, grad_out, mkeys, mvalues, ids, lengths, buckets, table,
         wq, wk, wv, gain1, grad_gain2):
    n, d = sz.rows, sz.width
    low = shape((n, d), BF16)
    first = d + sz.prefix * sz.entries
    mem = (sz.questions * sz.pad, sz.prefix * d)
    return pl.pallas_call(
        functools.partial(back_kernel, sz),
        in_specs=[SMEM] + [ANY] * 6 + [VMEM] * 3 + [SMEM] + [VMEM] * 2 + [ANY] * 3 + [VMEM] * 2,
        out_specs=[ANY] * 9,
        out_shape=[
            low,
            low,
            low,
            shape((first, d), F32),
            shape((d + SMALL, d), F32),
            shape((first // 2, d), F32),
            shape((first // 2, d), F32),
            shape(((d + SMALL) // 2, d), F32),
            shape(((d + SMALL) // 2, d), F32),
        ],
        scratch_shapes=[pltpu.VMEM((n, d), BF16)] * 5
        + [pltpu.VMEM((3, d, d), BF16)]
        + [pltpu.VMEM((n, d), BF16)] * 3
        + [
            pltpu.VMEM((2, first + d + SMALL, d), F32),
            pltpu.VMEM((sz.span, sz.heads * sz.seq), F32),
            pltpu.VMEM(mem, BF16),
            pltpu.VMEM(mem, BF16),
            pltpu.VMEM(mem, F32),
            pltpu.VMEM(mem, F32),
            pltpu.VMEM((sz.seq, sz.heads * sz.seq), F32),
            pltpu.VMEM((sz.buckets, sz.heads * sz.seq), F32),
            pltpu.SemaphoreType.DMA((9,)),
            pltpu.SemaphoreType.DMA((9,)),
        ],
        compiler_params=params(),
        cost_estimate=cost(step),
        name="back",
    )(core, query, key, value, d_att, normed1, grad_out, mkeys, mvalues, ids, lengths, buckets, table,
      wq, wk, wv, gain1, grad_gain2)


def last_kernel(tokens, d_hidden, gain1, d_query, d_key, d_value, wq, wk, wv, grad_tokens):
    d_normed = nt(d_query[...], wq[...])
    d_normed = d_normed + nt(d_key[...], wk[...])
    d_normed = d_normed + nt(d_value[...], wv[...])
    x = tokens[...].astype(F32)
    scale = lax.rsqrt(jnp.mean(x * x, axis=-1, keepdims=True) + EPS)
    base = x * scale
    scaled = d_normed * gain1[...].reshape(1, -1)
    back_in = scale * (scaled - base * jnp.mean(scaled * base, axis=-1, keepdims=True))
    grad_tokens[...] = (d_hidden[...] + back_in).astype(BF16)


def last(step, tokens, d_hidden, gain1, d_query, d_key, d_value, wq, wk, wv):
    n, d = tokens.shape
    rows = pl.BlockSpec((256, d), lambda j: (j, 0))
    square = pl.BlockSpec((d, d), lambda j: (0, 0))
    return pl.pallas_call(
        last_kernel,
        grid=(n // 256,),
        in_specs=[rows, rows, pl.BlockSpec((d,), lambda j: (0,))] + [rows] * 3 + [square] * 3,
        out_specs=rows,
        out_shape=shape((n, d), BF16),
        compiler_params=params(),
        cost_estimate=cost(step),
        name="last",
    )(tokens, d_hidden, gain1, d_query, d_key, d_value, wq, wk, wv)


def output_kernel(hidden, act, wo, out):
    out[...] = (hidden[...] + nn(act[...], wo[...])).astype(BF16)


def output(step, hidden, act, wo):
    n, d = hidden.shape
    units_all = act.shape[1]
    rows = pl.BlockSpec((256, d), lambda j: (j, 0))
    return pl.pallas_call(
        output_kernel,
        grid=(n // 256,),
        in_specs=[
            rows,
            pl.BlockSpec((256, units_all), lambda j: (j, 0)),
            pl.BlockSpec((units_all, d), lambda j: (0, 0)),
        ],
        out_specs=rows,
        out_shape=shape((n, d), BF16),
        compiler_params=params(),
        cost_estimate=cost(step),
        name="output",
    )(hidden, act, wo)


CORE = ("dp", 1)
LINK_Y = ("dp", 2)
LINK_X = ("grp", 1)
LINK_Z = ("dp", 4)


def swap(value, link, sizes):
    axis, stride = link
    return lax.ppermute(value, axis, [(i, i ^ stride) for i in range(sizes[axis])])


def bit_of(link):
    axis, stride = link
    return (lax.axis_index(axis) // stride) % 2


class Halves:
    def __init__(self, low, high):
        self.low, self.high = low, high


def add_split_kernel(layout, bits, *refs):
    refs = list(refs)
    outs = refs[-2 * len(layout) :]
    for i, halves in enumerate(layout):
        for out, value in ((outs[2 * i], bits[i]), (outs[2 * i + 1], 1 - bits[i])):
            one = refs.pop(0)[...]
            if halves:
                low, high = refs.pop(0), refs.pop(0)
                out[...] = one + jnp.where(value == 0, low[...], high[...])
            else:
                out[...] = one + refs.pop(0)[...]


def add_split(step, bits, parts):
    steps = 2
    in_specs, out_specs, outs, operands, layout = [], [], [], [], []
    for i, (kept, got) in enumerate(parts):
        rows, d = kept.shape
        rb = rows // 2 // steps
        block = pl.BlockSpec((rb, d), lambda j, b: (j, 0))
        layout.append(isinstance(got, Halves))
        for mine in (True, False):
            for array in (kept, got):
                if isinstance(array, Halves):
                    in_specs += [block, block]
                    operands += [array.low, array.high]
                    continue

                def index(j, b, i=i, mine=mine):
                    half = b[i] if mine else 1 - b[i]
                    return (half * steps + j, 0)

                in_specs.append(pl.BlockSpec((rb, d), index))
                operands.append(array)
            out_specs.append(block)
            outs.append(shape((rows // 2, d), F32))
    result = pl.pallas_call(
        functools.partial(add_split_kernel, layout),
        grid_spec=pltpu.PrefetchScalarGridSpec(
            num_scalar_prefetch=1, grid=(steps,), in_specs=in_specs, out_specs=out_specs
        ),
        out_shape=outs,
        compiler_params=params(),
        cost_estimate=cost(step),
        name="add_split",
    )(bits, *operands)
    return [(result[2 * i], result[2 * i + 1]) for i in range(len(parts))]


def add_pairs_kernel(a, b, c, d, out0, out1):
    out0[...] = a[...] + b[...]
    out1[...] = c[...] + d[...]


def add_pairs(step, a, b, c, d):
    return pl.pallas_call(
        add_pairs_kernel,
        in_specs=[VMEM] * 4,
        out_specs=[VMEM] * 2,
        out_shape=[shape(a.shape, F32), shape(c.shape, F32)],
        compiler_params=params(),
        cost_estimate=cost(step),
        name="add_pairs",
    )(a, b, c, d)


def z_split_kernel(bit, a, b, c, d, keep, send):
    at = 0
    for left, right in ((a, b), (c, d)):
        n = left.shape[0] // 2
        for out, half in ((keep, bit[0]), (send, 1 - bit[0])):
            rows = pl.ds(pl.multiple_of(half * n, 8), n)
            out[at : at + n, :] = left[rows, :] + right[rows, :]
        at += n


def z_split(step, bit, a, b, c, d):
    out = shape(((a.shape[0] + c.shape[0]) // 2, a.shape[1]), F32)
    return pl.pallas_call(
        z_split_kernel,
        in_specs=[SMEM] + [VMEM] * 4,
        out_specs=[VMEM] * 2,
        out_shape=[out, out],
        compiler_params=params(),
        cost_estimate=cost(step),
        name="z_split",
    )(bit, a, b, c, d)


def z_mixed_kernel(bit, a, b, c, d, whole, keep, send):
    whole[...] = a[...] + b[...]
    n = c.shape[0] // 2
    for out, half in ((keep, bit[0]), (send, 1 - bit[0])):
        rows = pl.ds(pl.multiple_of(half * n, 8), n)
        out[...] = c[rows, :] + d[rows, :]


def z_mixed(step, bit, a, b, c, d):
    half = shape((c.shape[0] // 2, c.shape[1]), F32)
    return pl.pallas_call(
        z_mixed_kernel,
        in_specs=[SMEM] + [VMEM] * 4,
        out_specs=[VMEM] * 3,
        out_shape=[shape(a.shape, F32), half, half],
        compiler_params=params(),
        cost_estimate=cost(step),
        name="z_mixed",
    )(bit, a, b, c, d)


def z_add_kernel(a, b, out):
    out[...] = a[...] + b[...]


def z_add(step, a, b):
    return pl.pallas_call(
        z_add_kernel,
        in_specs=[VMEM] * 2,
        out_specs=VMEM,
        out_shape=shape(a.shape, F32),
        compiler_params=params(),
        cost_estimate=cost(step),
        name="z_add",
    )(a, b)


def z_join_kernel(bit, own, got, *outs):
    at = 0
    for out in outs:
        n = out.shape[0] // 2
        out[pl.ds(pl.multiple_of(bit[0] * n, 8), n), :] = own[at : at + n, :]
        out[pl.ds(pl.multiple_of((1 - bit[0]) * n, 8), n), :] = got[at : at + n, :]
        at += n


def z_join(step, bit, own, got, rows):
    return pl.pallas_call(
        z_join_kernel,
        in_specs=[SMEM] + [VMEM] * 2,
        out_specs=[VMEM] * len(rows),
        out_shape=[shape((r, own.shape[1]), F32) for r in rows],
        compiler_params=params(),
        cost_estimate=cost(step),
        name="z_join",
    )(bit, own, got)


def join_kernel(bits, a, b, c, d, out0, out1, both):
    at = 0
    for first, own, got, out in ((0, a, b, out0), (1, c, d, out1)):
        n = own.shape[0]
        low = pl.multiple_of(bits[first] * n, 8)
        high = pl.multiple_of((1 - bits[first]) * n, 8)
        out[pl.ds(low, n), :] = own[...]
        out[pl.ds(high, n), :] = got[...]
        both[at : at + 2 * n, :] = out[...]
        at += 2 * n


def join(step, bits, a, b, c, d):
    wide = a.shape[1]
    rows = (2 * a.shape[0], 2 * c.shape[0])
    return pl.pallas_call(
        join_kernel,
        in_specs=[SMEM] + [VMEM] * 4,
        out_specs=[VMEM] * 3,
        out_shape=[shape((r, wide), F32) for r in rows + (sum(rows),)],
        compiler_params=params(),
        cost_estimate=cost(step),
        name="join",
    )(bits, a, b, c, d)


def rest_groups(size, low):
    return [[i for i in range(size) if i % low == r] for r in range(low)]


class Order:
    def __init__(self):
        self.done = None

    def after(self, value):
        if self.done is not None:
            value, _ = lax.optimization_barrier((value, self.done))
        return value

    def run(self, kernel, step, first, *rest):
        result = kernel(step, self.after(first), *rest)
        self.done = jax.tree.leaves(result)[0]
        return result

    def wait(self, *values):
        self.done = (self.done, values)


class Reduction:
    def __init__(self, name, order, sizes, turn_by, plan, outs):
        self.name, self.order, self.sizes, self.turn_by = name, order, sizes, turn_by
        self.plan, self.outs, self.placed = plan, outs, ()
        x_bit, y_bit = bit_of(LINK_X), bit_of(LINK_Y)
        self.xy = jnp.stack([x_bit, y_bit]).astype(jnp.int32)
        self.yx = jnp.stack([y_bit, x_bit]).astype(jnp.int32)
        self.z_bit = bit_of(LINK_Z).reshape(1).astype(jnp.int32)
        self.place_bits = jnp.stack([bit_of(CORE), x_bit, y_bit]).astype(jnp.int32)
        self.links = (LINK_X, LINK_Y)
        self.kept, self.got = [None, None], [None, None]

    def run(self, kernel, stage, first, *rest):
        return self.order.run(kernel, self.name + stage, first, *rest)

    def swap(self, value, link):
        return swap(self.order.after(value), link, self.sizes)

    def begin(self, part, keep, send):
        self.kept[part] = keep
        self.got[part] = Halves(*(self.swap(half, CORE) for half in send))

    def first(self, *which):
        def kernel(step, bits):
            return add_split(step, bits, [(self.kept[i], self.got[i]) for i in which])

        halves = self.run(kernel, "1", self.xy if which == (0, 1) else self.xy[which[0] :])
        for i, (keep, send) in zip(which, halves):
            self.kept[i], self.got[i] = keep, self.swap(send, self.links[i])

    def second(self):
        halves = self.run(add_split, "2", self.yx, list(zip(self.kept, self.got)))
        for i, (keep, send) in enumerate(halves):
            self.kept[i], self.got[i] = keep, self.swap(send, self.links[1 - i])

    def z_sum(self, values):
        groups = rest_groups(self.sizes["dp"], 4)
        groups = groups[self.turn_by :] + groups[: self.turn_by]
        values = lax.psum(values, "dp", axis_index_groups=groups)
        if self.sizes["grp"] > 2:
            values = lax.psum(values, "grp", axis_index_groups=rest_groups(self.sizes["grp"], 2))
        return list(values)

    def third(self):
        pair = self.run(add_pairs, "3", self.kept[0], self.got[0], self.kept[1], self.got[1])
        self.kept = self.z_sum(tuple(pair))

    def collect(self):
        self.order.wait(self.kept[0])

    def z_start(self, keep, send):
        self.kept, self.got = keep, self.swap(send, LINK_Z)
        self.rest = [("dp", 1 << k) for k in range(3, self.sizes["dp"].bit_length() - 1)]
        self.rest += [("grp", 1 << k) for k in range(1, self.sizes["grp"].bit_length() - 1)]

    def z_first(self):
        self.whole, self.rows = [], (self.kept[0].shape[0], self.kept[1].shape[0])
        self.z_start(*self.run(z_split, "3", self.z_bit, self.kept[0], self.got[0], self.kept[1], self.got[1]))

    def z_first_mixed(self):
        self.rows = (self.kept[1].shape[0],)
        whole, keep, send = self.run(
            z_mixed, "3", self.z_bit, self.kept[0], self.got[0], self.kept[1], self.got[1]
        )
        self.whole = self.z_sum((whole,))
        self.z_start(keep, send)

    def z_second(self):
        for link in self.rest:
            self.kept = self.run(z_add, "z1", self.kept, self.got)
            self.got = self.swap(self.kept, link)

    def z_third(self):
        self.kept = self.run(z_add, "z2", self.kept, self.got)
        self.got = self.swap(self.kept, LINK_Z)

    def z_fourth(self):
        parts = self.run(z_join, "z3", self.z_bit, self.kept, self.got, self.rows)
        self.kept = self.whole + list(parts)

    def fourth(self):
        self.got = [self.swap(self.kept[i], self.links[1 - i]) for i in (0, 1)]

    def fifth(self):
        g0, g1, both = self.run(join, "5", self.yx, self.kept[0], self.got[0], self.kept[1], self.got[1])
        self.near = (g0, g1)
        self.far = tuple(self.swap(self.near[i], self.links[i]) for i in (0, 1))
        self.both = both

    def cross_near(self):
        self.other_near = (self.swap(self.both, CORE),)

    def cross_near_apart(self):
        self.other_near = tuple(self.swap(g, CORE) for g in self.near)

    def sixth(self):
        self.far = tuple(self.order.after(v) for v in self.far)
        self.order.wait(*self.far)
        self.other_far = tuple(swap(v, CORE, self.sizes) for v in self.far)

    def place(self, flip, arrays):
        def kernel(step, bits):
            return place(step, flip, self.plan, bits, arrays, self.outs, self.placed)

        self.placed = self.run(kernel, "p", self.place_bits)

    def place_near(self):
        self.place(0, self.near + self.other_near)

    def place_far(self):
        self.place(1, self.far + self.other_far)


def place_kernel(flip, plan, n_in, n_out, n_alias, bits, *refs):
    srcs = refs[:n_in]
    outs = refs[n_in + n_alias : n_in + n_alias + n_out]
    bufs = refs[n_in + n_alias + n_out : -2]
    in_sems, out_sems = refs[-2:]
    loads = [pltpu.make_async_copy(srcs[i], bufs[i], in_sems.at[i]) for i in range(n_in)]
    for load in loads:
        load.start()
    for load in loads:
        load.wait()
    rows0 = bufs[0].shape[0]
    pieces = [(bufs[0], 0), (bufs[1], 0)]
    pieces += [(bufs[2], 0), (bufs[2], rows0)] if n_in == 3 else [(bufs[2], 0), (bufs[3], 0)]
    for core in (0, 1):
        for x_bit in (0, 1):
            for y_bit in (0, 1):
                test = (bits[0] == core) & (bits[1] == x_bit) & (bits[2] == y_bit)

                @pl.when(test)
                def _(core=core, x_bit=x_bit, y_bit=y_bit):
                    copies = []
                    for index, (buf, base) in enumerate(pieces):
                        other_core, part = index // 2, index % 2
                        key = (part, core ^ other_core, (x_bit, y_bit)[part] ^ flip)
                        for row, rows, out, where in plan[key]:
                            copies.append(
                                pltpu.make_async_copy(
                                    buf.at[pl.ds(base + row, rows)],
                                    outs[out].at[where],
                                    out_sems.at[len(copies)],
                                )
                            )
                    for copy in copies:
                        copy.start()
                    for copy in copies:
                        copy.wait()


def place(step, flip, plan, bits, arrays, outs, olds=()):
    n_copies = sum(len(v) for v in plan.values())
    return pl.pallas_call(
        functools.partial(place_kernel, flip, plan, len(arrays), len(outs), len(olds)),
        in_specs=[SMEM] + [ANY] * (len(arrays) + len(olds)),
        out_specs=[ANY] * len(outs),
        out_shape=outs,
        input_output_aliases={1 + len(arrays) + i: i for i in range(len(olds))},
        scratch_shapes=[pltpu.VMEM(a.shape, F32) for a in arrays]
        + [pltpu.SemaphoreType.DMA((len(arrays),)), pltpu.SemaphoreType.DMA((n_copies,))],
        compiler_params=params(),
        cost_estimate=cost(step),
        name="place",
    )(bits, *arrays, *olds)


def ffn_plan(first, d):
    plan = {}
    h = d // 2
    for part in (0, 1):
        at = (first + part) * d
        for half in (0, 1):
            plan[(part, 0, half)] = [(0, h, 0, (pl.ds(at + half * h, h), pl.ds(0, d)))]
            plan[(part, 1, half)] = [(0, h, 1, (pl.ds(half * h, h), pl.ds(at, d)))]
    return plan


def attn_plan(d, entries, prefix):
    plan = {}
    whole = pl.ds(0, d)
    for core, weight, mem in ((0, 0, 4), (1, 1, 5)):
        rows = d + prefix * entries
        h = rows // 2
        blocks = [(0, d, weight, 0)] + [(d + p * entries, entries, mem, p) for p in range(prefix)]
        for half in (0, 1):
            todo = []
            for start, count, out, p in blocks:
                low, high = max(start, half * h), min(start + count, (half + 1) * h)
                if low < high:
                    where = (pl.ds(low - start, high - low), pl.ds(p * d, d) if out >= 4 else whole)
                    todo.append((low - half * h, high - low, out, where))
            plan[(0, core, half)] = todo
    for core, blocks in ((0, [(0, d, 2), (d, SMALL, 6)]), (1, [(0, d, 3)])):
        h = (d + SMALL) // 2
        for half in (0, 1):
            todo = []
            for start, count, out in blocks:
                low, high = max(start, half * h), min(start + count, (half + 1) * h)
                if low < high:
                    todo.append((low - half * h, high - low, out, (pl.ds(low - start, high - low), whole)))
            plan[(1, core, half)] = todo
    return plan


def body(
    sizes,
    tokens,
    cotangent,
    w_query,
    w_key,
    w_value,
    w_attn_out,
    w_inner,
    w_outer,
    gain_attn,
    gain_ffn,
    bias_table,
    mem_keys,
    mem_values,
    mem_ids,
    lengths,
    buckets,
):
    questions, top = mem_ids.shape
    n, d = tokens.shape
    sz = Sizes(n, d, questions, bias_table.shape[1], bias_table.shape[0], mem_keys.shape[0], top, mem_keys.shape[1])
    table = bias_table.T
    core = bit_of(CORE).reshape(1).astype(jnp.int32)
    order = Order()
    square = shape((d, d), F32)
    mem = shape(mem_keys.shape, F32)
    ffn_outs = [shape(w_outer.shape, F32), shape(w_inner.shape, F32)]
    attn_outs = [square, square, square, square, mem, mem, shape((SMALL, d), F32)]
    red = {
        "A": Reduction("A", order, sizes, 0, ffn_plan(0, d), ffn_outs),
        "B": Reduction("B", order, sizes, 1, ffn_plan(2, d), ffn_outs),
        "C": Reduction("C", order, sizes, 2, attn_plan(d, sz.entries, sz.prefix), attn_outs),
    }
    v = {"wide": ()}

    def run_forward():
        names = ("normed1", "query", "key", "value", "attended", "hidden", "normed2")
        v.update(zip(names, order.run(
            lambda step, first, *rest: forward(step, sz, first, *rest), "fwd",
            tokens, w_query, w_key, w_value, w_attn_out, gain_attn, gain_ffn, table,
            mem_keys, mem_values, mem_ids, lengths, buckets,
        )))

    def run_units(q):
        v["wide"] = tuple(order.run(units, "e", v["normed2"], cotangent, w_inner, w_outer, q, v["wide"]))

    def run_weights(q):
        keep, *send = order.run(weights, "w", core, v["normed2"], cotangent, *v["wide"], q)
        red["AB"[q // 2]].begin(q % 2, keep, send)

    def run_mid():
        names = ("d_hidden", "d_attended", "grad_out", "grad_gain2")
        v.update(zip(names, order.run(
            mid, "mid", v["wide"][1], w_inner, v["hidden"], cotangent, gain_ffn, v["attended"], w_attn_out
        )))

    def run_back():
        names = ("d_query", "d_key", "d_value", "keep0", "keep1", "send00", "send01", "send10", "send11")
        v.update(zip(names, order.run(
            lambda step, first, *rest: back(step, sz, first, *rest), "back",
            core, v["query"], v["key"], v["value"], v["d_attended"], v["normed1"], v["grad_out"], mem_keys, mem_values,
            mem_ids, lengths, buckets, table, w_query, w_key, w_value, gain_attn, v["grad_gain2"],
        )))

    def run_last():
        v["grad_tokens"] = order.run(
            last, "last", tokens, v["d_hidden"], gain_attn, v["d_query"], v["d_key"], v["d_value"],
            w_query, w_key, w_value,
        )

    def run_output():
        v["out"] = order.run(output, "out", v["hidden"], v["wide"][0], w_outer)

    steps = {"fwd": run_forward, "mid": run_mid, "back": run_back, "last": run_last, "out": run_output}
    for q in range(4):
        steps["e%d" % q] = functools.partial(run_units, q)
        steps["w%d" % q] = functools.partial(run_weights, q)
    for name, r in red.items():
        steps.update({
            name + "1": functools.partial(r.first, 0, 1),
            name + "10": functools.partial(r.first, 0),
            name + "11": functools.partial(r.first, 1),
            name + "2": r.second, name + "3": r.third, name + "c": r.collect,
            name + "z0": r.z_first, name + "h0": r.z_first_mixed, name + "z1": r.z_second, name + "z2": r.z_third, name + "z3": r.z_fourth,
            name + "4": r.fourth, name + "5": r.fifth, name + "6": r.sixth, name + "n": r.cross_near, name + "m": r.cross_near_apart,
            name + "pn": r.place_near, name + "pf": r.place_far,
        })
    def begin_attention(part):
        red["C"].begin(part, v["keep%d" % part], (v["send%d0" % part], v["send%d1" % part]))

    for part in (0, 1):
        steps["Cb%d" % part] = functools.partial(begin_attention, part)

    def hand_over():
        red["B"].placed = red["A"].placed

    steps["AB"] = hand_over
    for step in PLAN:
        steps[step]()
    out, grad_tokens = v["out"], v["grad_tokens"]
    grad_w_outer, grad_w_inner = red["B"].placed
    gq, gk, gv, go, gmk, gmv, small = red["C"].placed
    return (
        out,
        grad_tokens,
        gq,
        gk,
        gv,
        go,
        grad_w_inner,
        grad_w_outer,
        small[0],
        small[1],
        small[2, : sz.heads * sz.buckets].reshape(sz.heads, sz.buckets).T,
        gmk,
        gmv,
    )


def solution(mesh):
    split = P(("grp", "dp"), None)
    placed = (split, split) + (P(),) * 11 + (split, P(("grp", "dp")), P())
    return jax.shard_map(
        functools.partial(body, dict(mesh.shape)),
        mesh=mesh,
        in_specs=placed,
        out_specs=(split, split) + (P(),) * 11,
        check_vma=False,
    )
```

```python
import functools

import jax
import jax.numpy as jnp
from jax import lax
from jax.experimental import pallas as pl
from jax.experimental.pallas import tpu as pltpu
from jax.sharding import PartitionSpec as P

EPS = 1e-06
NEG = -1000000000.0
F32 = jnp.float32
BF16 = jnp.bfloat16
GELU_C = 0.7978845608028654
GELU_A = 0.044715
SMALL = 64
UNIT_ROWS = 512
UNROLL_FORWARD = 8
UNROLL_BACK = 4
VMEM_LIMIT = 64 * 1024 * 1024
VMEM = pl.BlockSpec(memory_space=pltpu.VMEM)
SMEM = pl.BlockSpec(memory_space=pltpu.SMEM)
ANY = pl.BlockSpec(memory_space=pl.ANY)
PLAN = (
    "fwd", "e0", "w0", "e1", "w1", "e2", "A1", "e3", "mid", "w2", "w3", "A2", "B1", "back", "A3", "Cb0", "B2",
    "Cb1", "C10", "C11", "out", "Bz0", "last", "Bz1", "Ac", "A4", "C2", "A5", "Am", "Bz2", "C3", "Bz3", "B4",
    "A6", "Apn", "B5", "Apf", "Bn", "Cc", "C4", "AB", "B6", "C5", "Cn", "Bpf", "Cpn", "Bpn", "C6", "Cpf",
)

COSTS = {"A1": 6e+09, "A2": 6e+09, "Ap": 3e+09, "Az1": 1e+10, "B1": 4e+10, "B5": 2e+10, "Bz1": 3e+09, "Bz2": 2e+10, "C1": 2e+10, "Cz2": 6e+09, "back": 4e+10, "e": 1e+10, "last": 4e+10}


def cost(name):
    return pl.CostEstimate(flops=int(COSTS.get(name, 1)), bytes_accessed=1, transcendentals=0)


def nn(left, right):
    return lax.dot_general(left, right, (((1,), (0,)), ((), ())), preferred_element_type=F32)


def nt(left, right):
    return lax.dot_general(left, right, (((1,), (1,)), ((), ())), preferred_element_type=F32)


def tn(left, right):
    return lax.dot_general(left, right, (((0,), (0,)), ((), ())), preferred_element_type=F32)


class Copies:
    def __init__(self, sems):
        self.sems, self.made = sems, []

    def start(self, source, target):
        copy = pltpu.make_async_copy(source, target, self.sems.at[len(self.made)])
        copy.start()
        self.made.append(copy)
        return copy

    def wait(self):
        for copy in self.made:
            copy.wait()


def params():
    return pltpu.CompilerParams(vmem_limit_bytes=VMEM_LIMIT)


def shape(dims, dtype):
    return jax.ShapeDtypeStruct(dims, dtype)


class Sizes:
    def __init__(self, rows, width, questions, heads, buckets, entries, top, mem_width):
        self.rows = rows
        self.width = width
        self.questions = questions
        self.heads = heads
        self.buckets = buckets
        self.entries = entries
        self.top = top
        self.prefix = mem_width // width
        self.seq = rows // questions
        self.dh = width // heads
        self.pad = -(-top // 16) * 16
        self.span = self.seq + self.prefix * self.pad
        self.quad = 4
        self.qw = self.quad * self.dh
        self.quads = heads // self.quad


def head_mask(sz):
    n = sz.quad * sz.seq
    head = lax.broadcasted_iota(jnp.int32, (n, sz.qw), 0) // sz.seq
    lane = lax.broadcasted_iota(jnp.int32, (n, sz.qw), 1) // sz.dh
    return jnp.where(head == lane, 1.0, 0.0).astype(BF16)


def spread(block, mask, sz):
    return jnp.concatenate([block] * sz.quad, axis=0) * mask


def gather_diag(full, sz):
    s = sz.seq
    lane = lax.broadcasted_iota(jnp.int32, (s, 2 * sz.dh), 1)
    parts = []
    for pair in range(sz.quad // 2):
        cols = slice(pair * 2 * sz.dh, (pair + 1) * 2 * sz.dh)
        low = full[(2 * pair) * s : (2 * pair + 1) * s, cols]
        high = full[(2 * pair + 1) * s : (2 * pair + 2) * s, cols]
        parts.append(jnp.where(lane < sz.dh, low, high))
    return jnp.concatenate(parts, axis=1)


def bucket_lanes(buckets_ref, sz):
    row = lax.broadcasted_iota(jnp.int32, (sz.seq, 2 * sz.seq), 0)
    lane = lax.broadcasted_iota(jnp.int32, (sz.seq, 2 * sz.seq), 1)
    pick = jnp.where(lane % sz.seq == row, 1.0, 0.0).astype(BF16)
    return tn(buckets_ref[...].astype(F32).astype(BF16), pick)


def fill_bias(bias_ref, table_ref, buckets_ref, sz):
    bt = bucket_lanes(buckets_ref, sz)
    width = sz.heads * sz.seq
    head = lax.broadcasted_iota(jnp.int32, (sz.heads, width), 0)
    lane = lax.broadcasted_iota(jnp.int32, (sz.heads, width), 1) // sz.seq
    wide = lax.dot_general(
        table_ref[...], jnp.where(head == lane, 1.0, 0.0), (((0,), (0,)), ((), ())),
        precision=lax.Precision.HIGHEST, preferred_element_type=F32,
    )
    for pair in range(sz.heads // 2):
        cols = slice(pair * 2 * sz.seq, (pair + 1) * 2 * sz.seq)
        acc = jnp.zeros((sz.seq, 2 * sz.seq), F32)
        for b in range(sz.buckets):
            acc = jnp.where(bt == float(b), wide[b : b + 1, cols], acc)
        bias_ref[0 : sz.seq, cols] = acc
    n = sz.prefix * sz.pad
    row = lax.broadcasted_iota(jnp.int32, (n, sz.heads * sz.seq), 0) % sz.pad
    bias_ref[sz.seq :, :] = jnp.where(row < sz.top, 0.0, NEG)


def fill_memory(pick, table_ref, out_ref):
    out_ref[...] = nn(pick, table_ref[...]).astype(BF16)


def one_hot(ids_ref, sz):
    n = sz.questions * sz.pad
    row = lax.broadcasted_iota(jnp.int32, (n, sz.questions), 0) // sz.pad
    question = lax.broadcasted_iota(jnp.int32, (n, sz.questions), 1)
    repeat = jnp.where(row == question, 1.0, 0.0).astype(BF16)
    spread_ids = nn(repeat, (ids_ref[...] + 1).astype(F32).astype(BF16))
    slot = lax.broadcasted_iota(jnp.int32, (n, sz.top), 0) % sz.pad
    own = slot == lax.broadcasted_iota(jnp.int32, (n, sz.top), 1)
    column = jnp.sum(jnp.where(own, spread_ids, 0.0), axis=1, keepdims=True)
    lane = lax.broadcasted_iota(jnp.int32, (n, sz.entries), 1).astype(F32)
    return jnp.where(lane + 1.0 == column, 1.0, 0.0).astype(BF16)


def key_block(self_ref, mem_ref, q, col, sz):
    rows = pl.ds(pl.multiple_of(q * sz.seq, sz.seq), sz.seq)
    mrows = pl.ds(pl.multiple_of(q * sz.pad, sz.pad), sz.pad)
    parts = [self_ref[rows, col : col + sz.qw]]
    for p in range(sz.prefix):
        parts.append(mem_ref[mrows, p * sz.width + col : p * sz.width + col + sz.qw])
    return jnp.concatenate(parts, axis=0)


def probabilities(keys, spread_query, bias, length, sz):
    scores = nt(keys, spread_query) + bias
    row = lax.broadcasted_iota(jnp.int32, scores.shape, 0)
    admitted = jnp.logical_or(row < length, row >= sz.seq)
    scores = jnp.where(admitted, scores, NEG)
    top = jnp.max(scores, axis=0, keepdims=True)
    expd = jnp.exp(scores - top)
    return expd * (1.0 / jnp.sum(expd, axis=0, keepdims=True))


def forward_kernel(
    sz,
    tokens_hbm, wq_hbm, wk_hbm, wv_hbm, wo_hbm, gain1, gain2, table, mkeys, mvalues, ids, lengths, buckets,
    normed1_hbm, query_hbm, key_hbm, value_hbm, attended_hbm, hidden_hbm, normed2_hbm,
    tokens, weights, normed1, query, key, value, attended, hidden, normed2,
    bias, memk, memv, in_sems, out_sems,
):
    block = 256
    loads, stores = Copies(in_sems), Copies(out_sems)
    sources = [tokens_hbm, wq_hbm, wk_hbm, wv_hbm, wo_hbm]
    targets = [tokens] + [weights.at[i] for i in range(4)]
    loaded = [loads.start(a, b) for a, b in zip(sources, targets)]
    pick = one_hot(ids, sz)
    fill_memory(pick, mkeys, memk)
    fill_memory(pick, mvalues, memv)
    fill_bias(bias, table, buckets, sz)
    loaded[0].wait()
    for r in range(0, sz.rows, block):
        x = tokens[r : r + block, :].astype(F32)
        scale = lax.rsqrt(jnp.mean(x * x, axis=-1, keepdims=True) + EPS)
        low = (x * scale * gain1[...].reshape(1, -1)).astype(BF16)
        normed1[r : r + block, :] = low
    stores.start(normed1, normed1_hbm)
    for i, (out, out_hbm) in enumerate(((query, query_hbm), (key, key_hbm), (value, value_hbm))):
        loaded[1 + i].wait()
        for r in range(0, sz.rows, block):
            out[r : r + block, :] = nn(normed1[r : r + block, :], weights[i]).astype(BF16)
        stores.start(out, out_hbm)
    mask = head_mask(sz)

    def step(q, carry):
        length = lengths[q]
        rows = pl.ds(pl.multiple_of(q * sz.seq, sz.seq), sz.seq)
        for c in range(sz.quads):
            col = c * sz.qw
            sq = spread(query[rows, col : col + sz.qw], mask, sz)
            keys = key_block(key, memk, q, col, sz)
            values = key_block(value, memv, q, col, sz)
            probs = probabilities(keys, sq, bias[:, col : col + sz.qw], length, sz)
            full = tn(probs.astype(BF16), values)
            attended[rows, col : col + sz.qw] = gather_diag(full, sz).astype(BF16)
        return carry

    lax.fori_loop(0, sz.questions, step, 0, unroll=UNROLL_FORWARD)
    stores.start(attended, attended_hbm)
    loaded[4].wait()
    for r in range(0, sz.rows, block):
        rows = slice(r, r + block)
        h = tokens[rows, :].astype(F32) + nn(attended[rows, :], weights[3])
        hidden[rows, :] = h
        scale = lax.rsqrt(jnp.mean(h * h, axis=-1, keepdims=True) + EPS)
        normed2[rows, :] = (h * scale * gain2[...].reshape(1, -1)).astype(BF16)
        stores.start(hidden.at[pl.ds(r, block)], hidden_hbm.at[pl.ds(r, block)])
        stores.start(normed2.at[pl.ds(r, block)], normed2_hbm.at[pl.ds(r, block)])
    stores.wait()


def forward(step, sz, tokens, wq, wk, wv, wo, gain1, gain2, table, mkeys, mvalues, ids, lengths, buckets):
    n, d = sz.rows, sz.width
    low = shape((n, d), BF16)
    outs = [low, low, low, low, low, shape((n, d), F32), low]
    mem = (sz.questions * sz.pad, sz.prefix * d)
    return pl.pallas_call(
        functools.partial(forward_kernel, sz),
        in_specs=[ANY] * 5 + [VMEM] * 6 + [SMEM, VMEM],
        out_specs=[ANY] * 7,
        out_shape=outs,
        scratch_shapes=[pltpu.VMEM((n, d), BF16), pltpu.VMEM((4, d, d), BF16)]
        + [pltpu.VMEM(o.shape, o.dtype) for o in outs]
        + [
            pltpu.VMEM((sz.span, sz.heads * sz.seq), F32),
            pltpu.VMEM(mem, BF16),
            pltpu.VMEM(mem, BF16),
            pltpu.SemaphoreType.DMA((5,)),
            pltpu.SemaphoreType.DMA((5 + 2 * (n // 256),)),
        ],
        compiler_params=params(),
        cost_estimate=cost(step),
        name="forward",
    )(tokens, wq, wk, wv, wo, gain1, gain2, table, mkeys, mvalues, ids, lengths, buckets)


def unit_kernel(olds, normed2, cot, wi, wo, *refs):
    act, d_inner = refs[olds:]
    v = nn(normed2[...], wi[...])
    d_act = nt(cot[...], wo[...])
    sq = v * v
    t = jnp.tanh(v * (GELU_C + (GELU_C * GELU_A) * sq))
    half = 0.5 + 0.5 * t
    act[...] = (v * half).astype(BF16)
    slope = half + (0.5 * v) * (1.0 - t * t) * (GELU_C + (3.0 * GELU_C * GELU_A) * sq)
    d_inner[...] = (d_act * slope).astype(BF16)


def units(step, normed2, cot, wi, wo, quarter, olds=()):
    n, d = normed2.shape
    rows = pl.BlockSpec((UNIT_ROWS, d), lambda j: (j, 0))
    cols = pl.BlockSpec((UNIT_ROWS, d), lambda j: (j, quarter))
    wide = shape((n, wi.shape[1]), BF16)
    return pl.pallas_call(
        functools.partial(unit_kernel, len(olds)),
        grid=(n // UNIT_ROWS,),
        in_specs=[
            rows,
            rows,
            pl.BlockSpec((d, d), lambda j: (0, quarter)),
            pl.BlockSpec((d, d), lambda j: (quarter, 0)),
        ]
        + [ANY] * len(olds),
        out_specs=[cols, cols],
        out_shape=[wide, wide],
        input_output_aliases={4 + i: i for i in range(len(olds))},
        compiler_params=params(),
        cost_estimate=cost(step),
        name="units",
    )(normed2, cot, wi, wo, *olds)


def weight_kernel(quarter, extra, core, normed2_hbm, cot_hbm, act_hbm, d_inner_hbm, *refs):
    refs = list(refs)
    grad_out_hbm = refs.pop(0) if extra else None
    keep_hbm, send0_hbm, send1_hbm, normed2, cot, act, d_inner, keep, send, in_sems, out_sems = refs
    d = normed2.shape[1]
    h = d // 2
    cols = pl.ds(quarter * d, d)
    loads = Copies(in_sems)
    inner = [loads.start(normed2_hbm, normed2), loads.start(d_inner_hbm.at[:, cols], d_inner)]
    outer = [loads.start(act_hbm.at[:, cols], act), loads.start(cot_hbm, cot)]
    more = []
    if extra:
        for at, target in ((core[0], keep), (1 - core[0], send)):
            row = pl.multiple_of(at * h + quarter % 2 * extra, 8)
            more.append(loads.start(grad_out_hbm.at[pl.ds(row, extra)], target.at[pl.ds(d, extra)]))

    def write(first, second):
        stores = Copies(out_sems)
        for (ready, left, right), out in ((first, send), (second, keep)):
            for copy in ready:
                copy.wait()
            for i in (0, 1):
                half = slice(i * h, i * h + h)
                out[half, :] = tn(left[:, half], right[...])
            if out is send:
                for copy in more:
                    copy.wait()
                n = send0_hbm.shape[0]
                stores.start(send.at[pl.ds(0, n)], send0_hbm)
                stores.start(send.at[pl.ds(n, n)], send1_hbm)
        stores.start(keep, keep_hbm)
        stores.wait()

    @pl.when(core[0] == 0)
    def _():
        write((inner, normed2, d_inner), (outer, act, cot))

    @pl.when(core[0] != 0)
    def _():
        write((outer, act, cot), (inner, normed2, d_inner))


def weights(step, core, normed2, cot, act, d_inner, quarter, grad_out=None):
    n, d = normed2.shape
    extra = 0 if grad_out is None else d // 4
    rows = d + extra
    operands = (normed2, cot, act, d_inner) + (() if grad_out is None else (grad_out,))
    return pl.pallas_call(
        functools.partial(weight_kernel, quarter, extra),
        in_specs=[SMEM] + [ANY] * len(operands),
        out_specs=[ANY] * 3,
        out_shape=[shape((rows, d), F32)] + [shape((rows // 2, d), F32)] * 2,
        scratch_shapes=[pltpu.VMEM((n, d), BF16)] * 4
        + [pltpu.VMEM((rows, d), F32)] * 2
        + [pltpu.SemaphoreType.DMA((6,)), pltpu.SemaphoreType.DMA((3,))],
        compiler_params=params(),
        cost_estimate=cost(step),
        name="weights",
    )(core, *operands)


def mid_kernel(
    steps, d_in, wi, hidden_hbm, cot_hbm, gain2, attended_hbm, wo_hbm,
    d_hidden_hbm, d_attended_hbm, grad_out_hbm, grad_gain,
    total, hidden, cot, attended, wo, d_hidden, d_attended, grad_out, in_sems, out_sems,
):
    j = pl.program_id(0)
    block = 256
    n = hidden.shape[0]
    loads = ((hidden_hbm, hidden), (cot_hbm, cot), (wo_hbm, wo), (attended_hbm, attended))

    def load(i):
        return pltpu.make_async_copy(*loads[i], in_sems.at[i])

    @pl.when(j == 0)
    def _():
        for i in range(4):
            load(i).start()
        total[...] = nt(d_in[...], wi[...])

    @pl.when(j > 0)
    def _():
        total[...] += nt(d_in[...], wi[...])

    @pl.when(j == steps - 1)
    def _():
        stores = Copies(out_sems)
        for i in range(4):
            load(i).wait()
        acc = jnp.zeros((1, hidden.shape[1]), F32)
        for r in range(0, n, block):
            rows = slice(r, r + block)
            h = hidden[rows, :]
            scale = lax.rsqrt(jnp.mean(h * h, axis=-1, keepdims=True) + EPS)
            base = h * scale
            d_normed = total[rows, :]
            scaled = d_normed * gain2[...].reshape(1, -1)
            acc = acc + jnp.sum(d_normed * base, axis=0, keepdims=True)
            back = scale * (scaled - base * jnp.mean(scaled * base, axis=-1, keepdims=True))
            d_h = cot[rows, :].astype(F32) + back
            d_hidden[rows, :] = d_h
            low = d_h.astype(BF16)
            cot[rows, :] = low
            d_attended[rows, :] = nt(low, wo[...]).astype(BF16)
            where = pl.ds(r, block)
            stores.start(d_hidden.at[where], d_hidden_hbm.at[where])
            stores.start(d_attended.at[where], d_attended_hbm.at[where])
        grad_gain[...] = acc
        half = grad_out.shape[0] // 2
        for i in (0, 1):
            grad_out[i * half : (i + 1) * half, :] = tn(attended[:, i * half : (i + 1) * half], cot[...])
            where = pl.ds(i * half, half)
            stores.start(grad_out.at[where], grad_out_hbm.at[where])
        stores.wait()


def mid(step, d_in, wi, hidden, cot, gain2, attended, wo):
    n, d = hidden.shape
    steps = d_in.shape[1] // d
    return pl.pallas_call(
        functools.partial(mid_kernel, steps),
        grid=(steps,),
        in_specs=[
            pl.BlockSpec((n, d), lambda j: (0, j)),
            pl.BlockSpec((d, d), lambda j: (0, j)),
            ANY,
            ANY,
            pl.BlockSpec((d,), lambda j: (0,)),
            ANY,
            ANY,
        ],
        out_specs=[ANY, ANY, ANY, pl.BlockSpec((1, d), lambda j: (0, 0))],
        out_shape=[shape((n, d), F32), shape((n, d), BF16), shape((d, d), F32), shape((1, d), F32)],
        scratch_shapes=[
            pltpu.VMEM((n, d), F32),
            pltpu.VMEM((n, d), F32),
            pltpu.VMEM((n, d), BF16),
            pltpu.VMEM((n, d), BF16),
            pltpu.VMEM((d, d), BF16),
            pltpu.VMEM((n, d), F32),
            pltpu.VMEM((n, d), BF16),
            pltpu.VMEM((d, d), F32),
            pltpu.SemaphoreType.DMA((4,)),
            pltpu.SemaphoreType.DMA((2 * (n // 256) + 2,)),
        ],
        compiler_params=params(),
        cost_estimate=cost(step),
        name="mid",
    )(d_in, wi, hidden, cot, gain2, attended, wo)


def back_kernel(
    sz,
    my_core, query_hbm, key_hbm, value_hbm, d_att_hbm, normed1_hbm, mkeys, mvalues, ids, lengths, buckets,
    table, wq_hbm, wk_hbm, wv_hbm, gain1, grad_gain2,
    d_query_hbm, d_key_hbm, d_value_hbm, keep0_hbm, keep1_hbm, send00_hbm, send01_hbm, send10_hbm, send11_hbm,
    query, key, value, d_att, normed1, weights, d_query, d_key, d_value, shares,
    bias, memk, memv, d_memk, d_memv, d_bias, sums, in_sems, out_sems,
):
    d = sz.width
    h = d // 2
    loads, stores = Copies(in_sems), Copies(out_sems)
    early = [
        loads.start(a, b)
        for a, b in ((query_hbm, query), (key_hbm, key), (value_hbm, value), (d_att_hbm, d_att))
    ]
    late = [loads.start(normed1_hbm, normed1)]
    late += [loads.start(w, weights.at[i]) for i, w in enumerate((wq_hbm, wk_hbm, wv_hbm))]
    pick = one_hot(ids, sz)
    fill_memory(pick, mkeys, memk)
    fill_memory(pick, mvalues, memv)
    fill_bias(bias, table, buckets, sz)
    d_bias[...] = jnp.zeros_like(d_bias)
    mask = head_mask(sz)
    for copy in early:
        copy.wait()

    def step(q, carry):
        length = lengths[q]
        rows = pl.ds(pl.multiple_of(q * sz.seq, sz.seq), sz.seq)
        mrows = pl.ds(pl.multiple_of(q * sz.pad, sz.pad), sz.pad)
        for c in range(sz.quads):
            col = c * sz.qw
            cols = slice(col, col + sz.qw)
            sq = spread(query[rows, cols], mask, sz)
            so = spread(d_att[rows, cols], mask, sz)
            keys = key_block(key, memk, q, col, sz)
            values = key_block(value, memv, q, col, sz)
            probs = probabilities(keys, sq, bias[:, cols], length, sz)
            d_probs = nt(values, so)
            d_val = nn(probs.astype(BF16), so)
            inner = jnp.sum(probs * d_probs, axis=0, keepdims=True)
            d_scores = (probs * (d_probs - inner)).astype(BF16)
            d_bias[:, cols] += d_scores[0 : sz.seq, :].astype(F32)
            d_query[rows, cols] = gather_diag(tn(d_scores, keys), sz).astype(BF16)
            d_ky = nn(d_scores, sq)
            d_key[rows, cols] = d_ky[0 : sz.seq, :].astype(BF16)
            d_value[rows, cols] = d_val[0 : sz.seq, :].astype(BF16)
            for p in range(sz.prefix):
                part = slice(sz.seq + p * sz.pad, sz.seq + (p + 1) * sz.pad)
                to = slice(p * d + col, p * d + col + sz.qw)
                d_memk[mrows, to] = d_ky[part, :]
                d_memv[mrows, to] = d_val[part, :]
        return carry

    lax.fori_loop(0, sz.questions, step, 0, unroll=UNROLL_BACK)
    for a, b in ((d_query, d_query_hbm), (d_key, d_key_hbm), (d_value, d_value_hbm)):
        stores.start(a, b)
    for copy in late:
        copy.wait()

    mine, other = my_core[0], 1 - my_core[0]

    def store(start, keep, halves):
        stores.start(shares.at[mine, pl.ds(start, keep.shape[0])], keep)
        for half in halves:
            stores.start(shares.at[other, pl.ds(start, half.shape[0])], half)
            start += half.shape[0]

    def table_grad(full):
        high = full[...].astype(BF16)
        rest = (full[...] - high.astype(F32)).astype(BF16)
        return tn(pick, high) + tn(pick, rest)

    shares[0, 0:d, :] = tn(normed1[...], d_query[...])
    shares[1, 0:d, :] = tn(normed1[...], d_key[...])
    store(0, keep0_hbm, (send00_hbm, send01_hbm))
    for core, mem in ((0, d_memk), (1, d_memv)):
        shares[core, d : d + h, :] = tn(normed1[:, core * h : core * h + h], d_value[...])
        grads = table_grad(mem)
        for p in range(sz.prefix):
            rows = slice(d + h + p * sz.entries, d + h + (p + 1) * sz.entries)
            shares[core, rows, :] = grads[:, p * d : (p + 1) * d]

    bt = bucket_lanes(buckets, sz)
    for pair in range(sz.heads // 2):
        cols = slice(pair * 2 * sz.seq, (pair + 1) * 2 * sz.seq)
        part = d_bias[:, cols]
        for b in range(sz.buckets):
            sums[b : b + 1, cols] = jnp.sum(jnp.where(bt == float(b), part, 0.0), axis=0, keepdims=True)
    width = sz.heads * sz.seq
    flat = sz.heads * sz.buckets
    head_in = lax.broadcasted_iota(jnp.int32, (width, flat), 0) // sz.seq
    head_out = lax.broadcasted_iota(jnp.int32, (width, flat), 1) // sz.buckets
    by_head = jnp.dot(
        sums[...], jnp.where(head_in == head_out, 1.0, 0.0),
        precision=lax.Precision.HIGHEST, preferred_element_type=F32,
    )
    own = lax.broadcasted_iota(jnp.int32, (sz.buckets, flat), 0)
    lane = lax.broadcasted_iota(jnp.int32, (sz.buckets, flat), 1)
    bias_row = jnp.sum(jnp.where(lane % sz.buckets == own, by_head, 0.0), axis=0, keepdims=True)

    terms = weights[0].astype(F32) * shares[0, 0:d, :] + weights[1].astype(F32) * shares[1, 0:d, :]
    value_grad = jnp.concatenate([shares[0, d : d + h, :], shares[1, d : d + h, :]], axis=0)
    terms = terms + weights[2].astype(F32) * value_grad
    high = terms.astype(BF16)
    rest = (terms - high.astype(F32)).astype(BF16)
    ones = jnp.ones((8, d), BF16)
    total = (nt(ones, high) + nt(ones, rest))[0:1, :]
    small = d + h + sz.prefix * sz.entries
    shares[0, small : small + SMALL, :] = jnp.zeros((SMALL, d), F32)
    shares[1, small : small + SMALL, :] = jnp.zeros((SMALL, d), F32)
    shares[0, small : small + 1, :] = total / gain1[...].reshape(1, -1)
    shares[0, small + 1 : small + 2, :] = grad_gain2[...]
    shares[0, small + 2 : small + 3, 0:flat] = bias_row
    store(d, keep1_hbm, (send10_hbm, send11_hbm))
    stores.wait()


def back(step, sz, core, query, key, value, d_att, normed1, mkeys, mvalues, ids, lengths, buckets, table,
         wq, wk, wv, gain1, grad_gain2):
    n, d = sz.rows, sz.width
    low = shape((n, d), BF16)
    second = d // 2 + sz.prefix * sz.entries + SMALL
    mem = (sz.questions * sz.pad, sz.prefix * d)
    return pl.pallas_call(
        functools.partial(back_kernel, sz),
        in_specs=[SMEM] + [ANY] * 5 + [VMEM] * 3 + [SMEM] + [VMEM] * 2 + [ANY] * 3 + [VMEM] * 2,
        out_specs=[ANY] * 9,
        out_shape=[
            low,
            low,
            low,
            shape((d, d), F32),
            shape((second, d), F32),
            shape((d // 2, d), F32),
            shape((d // 2, d), F32),
            shape((second // 2, d), F32),
            shape((second // 2, d), F32),
        ],
        scratch_shapes=[pltpu.VMEM((n, d), BF16)] * 5
        + [pltpu.VMEM((3, d, d), BF16)]
        + [pltpu.VMEM((n, d), BF16)] * 3
        + [
            pltpu.VMEM((2, d + second, d), F32),
            pltpu.VMEM((sz.span, sz.heads * sz.seq), F32),
            pltpu.VMEM(mem, BF16),
            pltpu.VMEM(mem, BF16),
            pltpu.VMEM(mem, F32),
            pltpu.VMEM(mem, F32),
            pltpu.VMEM((sz.seq, sz.heads * sz.seq), F32),
            pltpu.VMEM((sz.buckets, sz.heads * sz.seq), F32),
            pltpu.SemaphoreType.DMA((8,)),
            pltpu.SemaphoreType.DMA((9,)),
        ],
        compiler_params=params(),
        cost_estimate=cost(step),
        name="back",
    )(core, query, key, value, d_att, normed1, mkeys, mvalues, ids, lengths, buckets, table,
      wq, wk, wv, gain1, grad_gain2)


def last_kernel(tokens, d_hidden, gain1, d_query, d_key, d_value, wq, wk, wv, grad_tokens):
    d_normed = nt(d_query[...], wq[...])
    d_normed = d_normed + nt(d_key[...], wk[...])
    d_normed = d_normed + nt(d_value[...], wv[...])
    x = tokens[...].astype(F32)
    scale = lax.rsqrt(jnp.mean(x * x, axis=-1, keepdims=True) + EPS)
    base = x * scale
    scaled = d_normed * gain1[...].reshape(1, -1)
    back_in = scale * (scaled - base * jnp.mean(scaled * base, axis=-1, keepdims=True))
    grad_tokens[...] = (d_hidden[...] + back_in).astype(BF16)


def last(step, tokens, d_hidden, gain1, d_query, d_key, d_value, wq, wk, wv):
    n, d = tokens.shape
    rows = pl.BlockSpec((256, d), lambda j: (j, 0))
    square = pl.BlockSpec((d, d), lambda j: (0, 0))
    return pl.pallas_call(
        last_kernel,
        grid=(n // 256,),
        in_specs=[rows, rows, pl.BlockSpec((d,), lambda j: (0,))] + [rows] * 3 + [square] * 3,
        out_specs=rows,
        out_shape=shape((n, d), BF16),
        compiler_params=params(),
        cost_estimate=cost(step),
        name="last",
    )(tokens, d_hidden, gain1, d_query, d_key, d_value, wq, wk, wv)


def output_kernel(hidden, act, wo, out):
    out[...] = (hidden[...] + nn(act[...], wo[...])).astype(BF16)


def output(step, hidden, act, wo):
    n, d = hidden.shape
    units_all = act.shape[1]
    rows = pl.BlockSpec((256, d), lambda j: (j, 0))
    return pl.pallas_call(
        output_kernel,
        grid=(n // 256,),
        in_specs=[
            rows,
            pl.BlockSpec((256, units_all), lambda j: (j, 0)),
            pl.BlockSpec((units_all, d), lambda j: (0, 0)),
        ],
        out_specs=rows,
        out_shape=shape((n, d), BF16),
        compiler_params=params(),
        cost_estimate=cost(step),
        name="output",
    )(hidden, act, wo)


CORE = ("dp", 1)
LINK_Y = ("dp", 2)
LINK_X = ("grp", 1)
LINK_Z = ("dp", 4)


def swap(value, link, sizes):
    axis, stride = link
    return lax.ppermute(value, axis, [(i, i ^ stride) for i in range(sizes[axis])])


def bit_of(link):
    axis, stride = link
    return (lax.axis_index(axis) // stride) % 2


class Halves:
    def __init__(self, low, high):
        self.low, self.high = low, high


def add_split_kernel(layout, bits, *refs):
    refs = list(refs)
    outs = refs[-2 * len(layout) :]
    for i, halves in enumerate(layout):
        for out, value in ((outs[2 * i], bits[i]), (outs[2 * i + 1], 1 - bits[i])):
            one = refs.pop(0)[...]
            if halves:
                low, high = refs.pop(0), refs.pop(0)
                out[...] = one + jnp.where(value == 0, low[...], high[...])
            else:
                out[...] = one + refs.pop(0)[...]


def add_split(step, bits, parts):
    steps = 2
    in_specs, out_specs, outs, operands, layout = [], [], [], [], []
    for i, (kept, got) in enumerate(parts):
        rows, d = kept.shape
        rb = rows // 2 // steps
        block = pl.BlockSpec((rb, d), lambda j, b: (j, 0))
        layout.append(isinstance(got, Halves))
        for mine in (True, False):
            for array in (kept, got):
                if isinstance(array, Halves):
                    in_specs += [block, block]
                    operands += [array.low, array.high]
                    continue

                def index(j, b, i=i, mine=mine):
                    half = b[i] if mine else 1 - b[i]
                    return (half * steps + j, 0)

                in_specs.append(pl.BlockSpec((rb, d), index))
                operands.append(array)
            out_specs.append(block)
            outs.append(shape((rows // 2, d), F32))
    result = pl.pallas_call(
        functools.partial(add_split_kernel, layout),
        grid_spec=pltpu.PrefetchScalarGridSpec(
            num_scalar_prefetch=1, grid=(steps,), in_specs=in_specs, out_specs=out_specs
        ),
        out_shape=outs,
        compiler_params=params(),
        cost_estimate=cost(step),
        name="add_split",
    )(bits, *operands)
    return [(result[2 * i], result[2 * i + 1]) for i in range(len(parts))]


def add_pairs_kernel(a, b, c, d, out0, out1):
    out0[...] = a[...] + b[...]
    out1[...] = c[...] + d[...]


def add_pairs(step, a, b, c, d):
    return pl.pallas_call(
        add_pairs_kernel,
        in_specs=[VMEM] * 4,
        out_specs=[VMEM] * 2,
        out_shape=[shape(a.shape, F32), shape(c.shape, F32)],
        compiler_params=params(),
        cost_estimate=cost(step),
        name="add_pairs",
    )(a, b, c, d)


def z_split_kernel(bit, a, b, c, d, keep, send):
    at = 0
    for left, right in ((a, b), (c, d)):
        n = left.shape[0] // 2
        for out, half in ((keep, bit[0]), (send, 1 - bit[0])):
            rows = pl.ds(pl.multiple_of(half * n, 8), n)
            out[at : at + n, :] = left[rows, :] + right[rows, :]
        at += n


def z_split(step, bit, a, b, c, d):
    out = shape(((a.shape[0] + c.shape[0]) // 2, a.shape[1]), F32)
    return pl.pallas_call(
        z_split_kernel,
        in_specs=[SMEM] + [VMEM] * 4,
        out_specs=[VMEM] * 2,
        out_shape=[out, out],
        compiler_params=params(),
        cost_estimate=cost(step),
        name="z_split",
    )(bit, a, b, c, d)


def z_mixed_kernel(bit, a, b, c, d, whole, keep, send):
    whole[...] = a[...] + b[...]
    n = c.shape[0] // 2
    for out, half in ((keep, bit[0]), (send, 1 - bit[0])):
        rows = pl.ds(pl.multiple_of(half * n, 8), n)
        out[...] = c[rows, :] + d[rows, :]


def z_mixed(step, bit, a, b, c, d):
    half = shape((c.shape[0] // 2, c.shape[1]), F32)
    return pl.pallas_call(
        z_mixed_kernel,
        in_specs=[SMEM] + [VMEM] * 4,
        out_specs=[VMEM] * 3,
        out_shape=[shape(a.shape, F32), half, half],
        compiler_params=params(),
        cost_estimate=cost(step),
        name="z_mixed",
    )(bit, a, b, c, d)


def z_add_kernel(a, b, out):
    out[...] = a[...] + b[...]


def z_add(step, a, b):
    return pl.pallas_call(
        z_add_kernel,
        in_specs=[VMEM] * 2,
        out_specs=VMEM,
        out_shape=shape(a.shape, F32),
        compiler_params=params(),
        cost_estimate=cost(step),
        name="z_add",
    )(a, b)


def z_join_kernel(bit, own, got, *outs):
    at = 0
    for out in outs:
        n = out.shape[0] // 2
        out[pl.ds(pl.multiple_of(bit[0] * n, 8), n), :] = own[at : at + n, :]
        out[pl.ds(pl.multiple_of((1 - bit[0]) * n, 8), n), :] = got[at : at + n, :]
        at += n


def z_join(step, bit, own, got, rows):
    return pl.pallas_call(
        z_join_kernel,
        in_specs=[SMEM] + [VMEM] * 2,
        out_specs=[VMEM] * len(rows),
        out_shape=[shape((r, own.shape[1]), F32) for r in rows],
        compiler_params=params(),
        cost_estimate=cost(step),
        name="z_join",
    )(bit, own, got)


def join_kernel(bits, a, b, c, d, out0, out1, both):
    at = 0
    for first, own, got, out in ((0, a, b, out0), (1, c, d, out1)):
        n = own.shape[0]
        low = pl.multiple_of(bits[first] * n, 8)
        high = pl.multiple_of((1 - bits[first]) * n, 8)
        out[pl.ds(low, n), :] = own[...]
        out[pl.ds(high, n), :] = got[...]
        both[at : at + 2 * n, :] = out[...]
        at += 2 * n


def join(step, bits, a, b, c, d):
    wide = a.shape[1]
    rows = (2 * a.shape[0], 2 * c.shape[0])
    return pl.pallas_call(
        join_kernel,
        in_specs=[SMEM] + [VMEM] * 4,
        out_specs=[VMEM] * 3,
        out_shape=[shape((r, wide), F32) for r in rows + (sum(rows),)],
        compiler_params=params(),
        cost_estimate=cost(step),
        name="join",
    )(bits, a, b, c, d)


def rest_groups(size, low):
    return [[i for i in range(size) if i % low == r] for r in range(low)]


class Order:
    def __init__(self):
        self.done = None

    def after(self, value):
        if self.done is not None:
            value, _ = lax.optimization_barrier((value, self.done))
        return value

    def run(self, kernel, step, first, *rest):
        result = kernel(step, self.after(first), *rest)
        self.done = jax.tree.leaves(result)[0]
        return result

    def wait(self, *values):
        self.done = (self.done, values)


class Reduction:
    def __init__(self, name, order, sizes, turn_by, plan, outs):
        self.name, self.order, self.sizes, self.turn_by = name, order, sizes, turn_by
        self.plan, self.outs, self.placed = plan, outs, ()
        x_bit, y_bit = bit_of(LINK_X), bit_of(LINK_Y)
        self.xy = jnp.stack([x_bit, y_bit]).astype(jnp.int32)
        self.yx = jnp.stack([y_bit, x_bit]).astype(jnp.int32)
        self.z_bit = bit_of(LINK_Z).reshape(1).astype(jnp.int32)
        self.place_bits = jnp.stack([bit_of(CORE), x_bit, y_bit]).astype(jnp.int32)
        self.links = (LINK_X, LINK_Y)
        self.kept, self.got = [None, None], [None, None]

    def run(self, kernel, stage, first, *rest):
        return self.order.run(kernel, self.name + stage, first, *rest)

    def swap(self, value, link):
        return swap(self.order.after(value), link, self.sizes)

    def begin(self, part, keep, send):
        self.kept[part] = keep
        self.got[part] = Halves(*(self.swap(half, CORE) for half in send))

    def first(self, *which):
        def kernel(step, bits):
            return add_split(step, bits, [(self.kept[i], self.got[i]) for i in which])

        halves = self.run(kernel, "1", self.xy if which == (0, 1) else self.xy[which[0] :])
        for i, (keep, send) in zip(which, halves):
            self.kept[i], self.got[i] = keep, self.swap(send, self.links[i])

    def second(self):
        halves = self.run(add_split, "2", self.yx, list(zip(self.kept, self.got)))
        for i, (keep, send) in enumerate(halves):
            self.kept[i], self.got[i] = keep, self.swap(send, self.links[1 - i])

    def z_sum(self, values):
        groups = rest_groups(self.sizes["dp"], 4)
        groups = groups[self.turn_by :] + groups[: self.turn_by]
        values = lax.psum(values, "dp", axis_index_groups=groups)
        if self.sizes["grp"] > 2:
            values = lax.psum(values, "grp", axis_index_groups=rest_groups(self.sizes["grp"], 2))
        return list(values)

    def third(self):
        pair = self.run(add_pairs, "3", self.kept[0], self.got[0], self.kept[1], self.got[1])
        self.kept = self.z_sum(tuple(pair))

    def collect(self):
        self.order.wait(self.kept[0])

    def z_start(self, keep, send):
        self.kept, self.got = keep, self.swap(send, LINK_Z)
        self.rest = [("dp", 1 << k) for k in range(3, self.sizes["dp"].bit_length() - 1)]
        self.rest += [("grp", 1 << k) for k in range(1, self.sizes["grp"].bit_length() - 1)]

    def z_first(self):
        self.whole, self.rows = [], (self.kept[0].shape[0], self.kept[1].shape[0])
        self.z_start(*self.run(z_split, "3", self.z_bit, self.kept[0], self.got[0], self.kept[1], self.got[1]))

    def z_first_mixed(self):
        self.rows = (self.kept[1].shape[0],)
        whole, keep, send = self.run(
            z_mixed, "3", self.z_bit, self.kept[0], self.got[0], self.kept[1], self.got[1]
        )
        self.whole = self.z_sum((whole,))
        self.z_start(keep, send)

    def z_second(self):
        for link in self.rest:
            self.kept = self.run(z_add, "z1", self.kept, self.got)
            self.got = self.swap(self.kept, link)

    def z_third(self):
        self.kept = self.run(z_add, "z2", self.kept, self.got)
        self.got = self.swap(self.kept, LINK_Z)

    def z_fourth(self):
        parts = self.run(z_join, "z3", self.z_bit, self.kept, self.got, self.rows)
        self.kept = self.whole + list(parts)

    def fourth(self):
        self.got = [self.swap(self.kept[i], self.links[1 - i]) for i in (0, 1)]

    def fifth(self):
        g0, g1, both = self.run(join, "5", self.yx, self.kept[0], self.got[0], self.kept[1], self.got[1])
        self.near = (g0, g1)
        self.far = tuple(self.swap(self.near[i], self.links[i]) for i in (0, 1))
        self.both = both

    def cross_near(self):
        self.other_near = (self.swap(self.both, CORE),)

    def cross_near_apart(self):
        self.other_near = tuple(self.swap(g, CORE) for g in self.near)

    def sixth(self):
        self.far = tuple(self.order.after(v) for v in self.far)
        self.order.wait(*self.far)
        self.other_far = tuple(swap(v, CORE, self.sizes) for v in self.far)

    def place(self, flip, arrays):
        def kernel(step, bits):
            return place(step, flip, self.plan, bits, arrays, self.outs, self.placed)

        self.placed = self.run(kernel, "p", self.place_bits)

    def place_near(self):
        self.place(0, self.near + self.other_near)

    def place_far(self):
        self.place(1, self.far + self.other_far)


def place_kernel(flip, plan, n_in, n_out, n_alias, bits, *refs):
    srcs = refs[:n_in]
    outs = refs[n_in + n_alias : n_in + n_alias + n_out]
    bufs = refs[n_in + n_alias + n_out : -2]
    in_sems, out_sems = refs[-2:]
    loads = [pltpu.make_async_copy(srcs[i], bufs[i], in_sems.at[i]) for i in range(n_in)]
    for load in loads:
        load.start()
    rows0 = bufs[0].shape[0]
    pieces = [(0, 0), (1, 0), (2, 0)] + [(2, rows0) if n_in == 3 else (3, 0)]
    for core in (0, 1):
        for x_bit in (0, 1):
            for y_bit in (0, 1):
                test = (bits[0] == core) & (bits[1] == x_bit) & (bits[2] == y_bit)

                @pl.when(test)
                def _(core=core, x_bit=x_bit, y_bit=y_bit):
                    copies = []
                    for index, (buf, base) in enumerate(pieces):
                        if base == 0:
                            loads[buf].wait()
                        other_core, part = index // 2, index % 2
                        key = (part, core ^ other_core, (x_bit, y_bit)[part] ^ flip)
                        for row, rows, out, where in plan[key]:
                            copies.append(
                                pltpu.make_async_copy(
                                    bufs[buf].at[pl.ds(base + row, rows)],
                                    outs[out].at[where],
                                    out_sems.at[len(copies)],
                                )
                            )
                            copies[-1].start()
                    for copy in copies:
                        copy.wait()


def place(step, flip, plan, bits, arrays, outs, olds=()):
    n_copies = 4 * max(len(v) for v in plan.values())
    return pl.pallas_call(
        functools.partial(place_kernel, flip, plan, len(arrays), len(outs), len(olds)),
        in_specs=[SMEM] + [ANY] * (len(arrays) + len(olds)),
        out_specs=[ANY] * len(outs),
        out_shape=outs,
        input_output_aliases={1 + len(arrays) + i: i for i in range(len(olds))},
        scratch_shapes=[pltpu.VMEM(a.shape, F32) for a in arrays]
        + [pltpu.SemaphoreType.DMA((len(arrays),)), pltpu.SemaphoreType.DMA((n_copies,))],
        compiler_params=params(),
        cost_estimate=cost(step),
        name="place",
    )(bits, *arrays, *olds)


def split_plan(rows, blocks):
    h = rows // 2
    plan = []
    for half in (0, 1):
        todo = []
        for start, count, out, row, cols in blocks:
            low, high = max(start, half * h), min(start + count, (half + 1) * h)
            if low < high:
                todo.append((low - half * h, high - low, out, (pl.ds(row + low - start, high - low), cols)))
        plan.append(todo)
    return plan


def ffn_plan(first, d, extra=0):
    plan = {}
    whole = pl.ds(0, d)
    for part in (0, 1):
        at = (first + part) * d
        for core, block in ((0, (0, d, 0, at, whole)), (1, (0, d, 1, 0, pl.ds(at, d)))):
            blocks = [block]
            if extra:
                blocks.append((d, extra, 2, core * d // 2 + part * extra, whole))
            for half, todo in enumerate(split_plan(d + extra, blocks)):
                plan[(part, core, half)] = todo
    return plan


def attn_plan(d, entries, prefix):
    plan = {}
    whole = pl.ds(0, d)
    h = d // 2
    small = h + prefix * entries
    for core in (0, 1):
        blocks = [(0, h, 2, core * h, whole)]
        blocks += [(h + p * entries, entries, 3 + core, 0, pl.ds(p * d, d)) for p in range(prefix)]
        if core == 0:
            blocks.append((small, SMALL, 5, 0, whole))
        for half, todo in enumerate(split_plan(d, [(0, d, core, 0, whole)])):
            plan[(0, core, half)] = todo
        for half, todo in enumerate(split_plan(small + SMALL, blocks)):
            plan[(1, core, half)] = todo
    return plan


def body(
    sizes,
    tokens,
    cotangent,
    w_query,
    w_key,
    w_value,
    w_attn_out,
    w_inner,
    w_outer,
    gain_attn,
    gain_ffn,
    bias_table,
    mem_keys,
    mem_values,
    mem_ids,
    lengths,
    buckets,
):
    questions, top = mem_ids.shape
    n, d = tokens.shape
    sz = Sizes(n, d, questions, bias_table.shape[1], bias_table.shape[0], mem_keys.shape[0], top, mem_keys.shape[1])
    table = bias_table.T
    core = bit_of(CORE).reshape(1).astype(jnp.int32)
    order = Order()
    square = shape((d, d), F32)
    mem = shape(mem_keys.shape, F32)
    ffn_outs = [shape(w_outer.shape, F32), shape(w_inner.shape, F32)]
    attn_outs = [square, square, square, mem, mem, shape((SMALL, d), F32)]
    red = {
        "A": Reduction("A", order, sizes, 0, ffn_plan(0, d), ffn_outs),
        "B": Reduction("B", order, sizes, 1, ffn_plan(2, d, d // 4), ffn_outs + [square]),
        "C": Reduction("C", order, sizes, 2, attn_plan(d, sz.entries, sz.prefix), attn_outs),
    }
    v = {"wide": ()}

    def run_forward():
        names = ("normed1", "query", "key", "value", "attended", "hidden", "normed2")
        v.update(zip(names, order.run(
            lambda step, first, *rest: forward(step, sz, first, *rest), "fwd",
            tokens, w_query, w_key, w_value, w_attn_out, gain_attn, gain_ffn, table,
            mem_keys, mem_values, mem_ids, lengths, buckets,
        )))

    def run_units(q):
        v["wide"] = tuple(order.run(units, "e", v["normed2"], cotangent, w_inner, w_outer, q, v["wide"]))

    def run_weights(q):
        grad_out = v["grad_out"] if q >= 2 else None
        keep, *send = order.run(weights, "w", core, v["normed2"], cotangent, *v["wide"], q, grad_out)
        red["AB"[q // 2]].begin(q % 2, keep, send)

    def run_mid():
        names = ("d_hidden", "d_attended", "grad_out", "grad_gain2")
        v.update(zip(names, order.run(
            mid, "mid", v["wide"][1], w_inner, v["hidden"], cotangent, gain_ffn, v["attended"], w_attn_out
        )))

    def run_back():
        names = ("d_query", "d_key", "d_value", "keep0", "keep1", "send00", "send01", "send10", "send11")
        v.update(zip(names, order.run(
            lambda step, first, *rest: back(step, sz, first, *rest), "back",
            core, v["query"], v["key"], v["value"], v["d_attended"], v["normed1"], mem_keys, mem_values,
            mem_ids, lengths, buckets, table, w_query, w_key, w_value, gain_attn, v["grad_gain2"],
        )))

    def run_last():
        v["grad_tokens"] = order.run(
            last, "last", tokens, v["d_hidden"], gain_attn, v["d_query"], v["d_key"], v["d_value"],
            w_query, w_key, w_value,
        )

    def run_output():
        v["out"] = order.run(output, "out", v["hidden"], v["wide"][0], w_outer)

    steps = {"fwd": run_forward, "mid": run_mid, "back": run_back, "last": run_last, "out": run_output}
    for q in range(4):
        steps["e%d" % q] = functools.partial(run_units, q)
        steps["w%d" % q] = functools.partial(run_weights, q)
    for name, r in red.items():
        steps.update({
            name + "1": functools.partial(r.first, 0, 1),
            name + "10": functools.partial(r.first, 0),
            name + "11": functools.partial(r.first, 1),
            name + "2": r.second, name + "3": r.third, name + "c": r.collect,
            name + "z0": r.z_first, name + "h0": r.z_first_mixed, name + "z1": r.z_second, name + "z2": r.z_third, name + "z3": r.z_fourth,
            name + "4": r.fourth, name + "5": r.fifth, name + "6": r.sixth, name + "n": r.cross_near, name + "m": r.cross_near_apart,
            name + "pn": r.place_near, name + "pf": r.place_far,
        })
    def begin_attention(part):
        red["C"].begin(part, v["keep%d" % part], (v["send%d0" % part], v["send%d1" % part]))

    for part in (0, 1):
        steps["Cb%d" % part] = functools.partial(begin_attention, part)

    def hand_over():
        red["B"].placed = red["A"].placed

    steps["AB"] = hand_over
    for step in PLAN:
        steps[step]()
    out, grad_tokens = v["out"], v["grad_tokens"]
    grad_w_outer, grad_w_inner, go = red["B"].placed
    gq, gk, gv, gmk, gmv, small = red["C"].placed
    return (
        out,
        grad_tokens,
        gq,
        gk,
        gv,
        go,
        grad_w_inner,
        grad_w_outer,
        small[0],
        small[1],
        small[2, : sz.heads * sz.buckets].reshape(sz.heads, sz.buckets).T,
        gmk,
        gmv,
    )


def solution(mesh):
    split = P(("grp", "dp"), None)
    placed = (split, split) + (P(),) * 11 + (split, P(("grp", "dp")), P())
    return jax.shard_map(
        functools.partial(body, dict(mesh.shape)),
        mesh=mesh,
        in_specs=placed,
        out_specs=(split, split) + (P(),) * 11,
        check_vma=False,
    )
```

```python
import functools

import jax
import jax.numpy as jnp
from jax import lax
from jax.experimental import pallas as pl
from jax.experimental.pallas import tpu as pltpu
from jax.sharding import PartitionSpec as P

EPS = 1e-06
NEG = -1000000000.0
F32 = jnp.float32
BF16 = jnp.bfloat16
GELU_C = 0.7978845608028654
GELU_A = 0.044715
SMALL = 64
UNIT_ROWS = 512
UNROLL_FORWARD = 8
UNROLL_BACK = 4
VMEM_LIMIT = 64 * 1024 * 1024
VMEM = pl.BlockSpec(memory_space=pltpu.VMEM)
SMEM = pl.BlockSpec(memory_space=pltpu.SMEM)
ANY = pl.BlockSpec(memory_space=pl.ANY)
PLAN = (
    "fwd", "e0", "e1", "w0", "w1", "e2", "A1", "e3", "mid", "w2", "w3", "A2", "B1", "back", "A3", "Cb0", "B2",
    "Cb1", "C10", "C11", "out", "Bz0", "last", "Bz1", "Ac", "A4", "C2", "A5", "Am", "Bz2", "C3", "Bz3", "B4",
    "A6", "Apn", "B5", "Apf", "Bn", "Cc", "C4", "AB", "B6", "C5", "Cm", "Bpf", "Cpn", "Bpn", "C6", "Cpf",
)

COSTS = {"A1": 6e+09, "A2": 6e+09, "Ap": 3e+09, "Az1": 1e+10, "B1": 4e+10, "B5": 2e+10, "Bz1": 3e+09, "Bz2": 2e+10, "C1": 2e+10, "C5": 4e+10, "Cz2": 6e+09, "back": 4e+10, "e": 1e+10, "last": 4e+10}


def cost(name):
    return pl.CostEstimate(flops=int(COSTS.get(name, 1)), bytes_accessed=1, transcendentals=0)


def nn(left, right):
    return lax.dot_general(left, right, (((1,), (0,)), ((), ())), preferred_element_type=F32)


def nt(left, right):
    return lax.dot_general(left, right, (((1,), (1,)), ((), ())), preferred_element_type=F32)


def tn(left, right):
    return lax.dot_general(left, right, (((0,), (0,)), ((), ())), preferred_element_type=F32)


class Copies:
    def __init__(self, sems):
        self.sems, self.made = sems, []

    def start(self, source, target):
        copy = pltpu.make_async_copy(source, target, self.sems.at[len(self.made)])
        copy.start()
        self.made.append(copy)
        return copy

    def wait(self):
        for copy in self.made:
            copy.wait()


def params():
    return pltpu.CompilerParams(vmem_limit_bytes=VMEM_LIMIT)


def shape(dims, dtype):
    return jax.ShapeDtypeStruct(dims, dtype)


class Sizes:
    def __init__(self, rows, width, questions, heads, buckets, entries, top, mem_width):
        self.rows = rows
        self.width = width
        self.questions = questions
        self.heads = heads
        self.buckets = buckets
        self.entries = entries
        self.top = top
        self.prefix = mem_width // width
        self.seq = rows // questions
        self.dh = width // heads
        self.pad = -(-top // 16) * 16
        self.span = self.seq + self.prefix * self.pad
        self.quad = 4
        self.qw = self.quad * self.dh
        self.quads = heads // self.quad


def head_mask(sz):
    n = sz.quad * sz.seq
    head = lax.broadcasted_iota(jnp.int32, (n, sz.qw), 0) // sz.seq
    lane = lax.broadcasted_iota(jnp.int32, (n, sz.qw), 1) // sz.dh
    return jnp.where(head == lane, 1.0, 0.0).astype(BF16)


def spread(block, mask, sz):
    return jnp.concatenate([block] * sz.quad, axis=0) * mask


def gather_diag(full, sz):
    s = sz.seq
    lane = lax.broadcasted_iota(jnp.int32, (s, 2 * sz.dh), 1)
    parts = []
    for pair in range(sz.quad // 2):
        cols = slice(pair * 2 * sz.dh, (pair + 1) * 2 * sz.dh)
        low = full[(2 * pair) * s : (2 * pair + 1) * s, cols]
        high = full[(2 * pair + 1) * s : (2 * pair + 2) * s, cols]
        parts.append(jnp.where(lane < sz.dh, low, high))
    return jnp.concatenate(parts, axis=1)


def bucket_lanes(buckets_ref, sz):
    row = lax.broadcasted_iota(jnp.int32, (sz.seq, 2 * sz.seq), 0)
    lane = lax.broadcasted_iota(jnp.int32, (sz.seq, 2 * sz.seq), 1)
    pick = jnp.where(lane % sz.seq == row, 1.0, 0.0).astype(BF16)
    return tn(buckets_ref[...].astype(F32).astype(BF16), pick)


def fill_bias(bias_ref, table_ref, buckets_ref, sz):
    bt = bucket_lanes(buckets_ref, sz)
    width = sz.heads * sz.seq
    head = lax.broadcasted_iota(jnp.int32, (sz.heads, width), 0)
    lane = lax.broadcasted_iota(jnp.int32, (sz.heads, width), 1) // sz.seq
    wide = lax.dot_general(
        table_ref[...], jnp.where(head == lane, 1.0, 0.0), (((0,), (0,)), ((), ())),
        precision=lax.Precision.HIGHEST, preferred_element_type=F32,
    )
    for pair in range(sz.heads // 2):
        cols = slice(pair * 2 * sz.seq, (pair + 1) * 2 * sz.seq)
        acc = jnp.zeros((sz.seq, 2 * sz.seq), F32)
        for b in range(sz.buckets):
            acc = jnp.where(bt == float(b), wide[b : b + 1, cols], acc)
        bias_ref[0 : sz.seq, cols] = acc
    n = sz.prefix * sz.pad
    row = lax.broadcasted_iota(jnp.int32, (n, sz.heads * sz.seq), 0) % sz.pad
    bias_ref[sz.seq :, :] = jnp.where(row < sz.top, 0.0, NEG)


def fill_memory(pick, table_ref, out_ref):
    out_ref[...] = nn(pick, table_ref[...]).astype(BF16)


def one_hot(ids_ref, sz):
    n = sz.questions * sz.pad
    row = lax.broadcasted_iota(jnp.int32, (n, sz.questions), 0) // sz.pad
    question = lax.broadcasted_iota(jnp.int32, (n, sz.questions), 1)
    repeat = jnp.where(row == question, 1.0, 0.0).astype(BF16)
    spread_ids = nn(repeat, (ids_ref[...] + 1).astype(F32).astype(BF16))
    slot = lax.broadcasted_iota(jnp.int32, (n, sz.top), 0) % sz.pad
    own = slot == lax.broadcasted_iota(jnp.int32, (n, sz.top), 1)
    column = jnp.sum(jnp.where(own, spread_ids, 0.0), axis=1, keepdims=True)
    lane = lax.broadcasted_iota(jnp.int32, (n, sz.entries), 1).astype(F32)
    return jnp.where(lane + 1.0 == column, 1.0, 0.0).astype(BF16)


def key_block(self_ref, mem_ref, q, col, sz):
    rows = pl.ds(pl.multiple_of(q * sz.seq, sz.seq), sz.seq)
    mrows = pl.ds(pl.multiple_of(q * sz.pad, sz.pad), sz.pad)
    parts = [self_ref[rows, col : col + sz.qw]]
    for p in range(sz.prefix):
        parts.append(mem_ref[mrows, p * sz.width + col : p * sz.width + col + sz.qw])
    return jnp.concatenate(parts, axis=0)


def probabilities(keys, spread_query, bias, length, sz):
    scores = nt(keys, spread_query) + bias
    row = lax.broadcasted_iota(jnp.int32, scores.shape, 0)
    admitted = jnp.logical_or(row < length, row >= sz.seq)
    scores = jnp.where(admitted, scores, NEG)
    top = jnp.max(scores, axis=0, keepdims=True)
    expd = jnp.exp(scores - top)
    return expd * (1.0 / jnp.sum(expd, axis=0, keepdims=True))


def forward_kernel(
    sz,
    tokens_hbm, wq_hbm, wk_hbm, wv_hbm, wo_hbm, gain1, gain2, table, mkeys, mvalues, ids, lengths, buckets,
    normed1_hbm, query_hbm, key_hbm, value_hbm, attended_hbm, hidden_hbm, normed2_hbm,
    tokens, weights, normed1, query, key, value, attended, hidden, normed2,
    bias, memk, memv, in_sems, out_sems,
):
    block = 256
    loads, stores = Copies(in_sems), Copies(out_sems)
    sources = [tokens_hbm, wq_hbm, wk_hbm, wv_hbm, wo_hbm]
    targets = [tokens] + [weights.at[i] for i in range(4)]
    loaded = [loads.start(a, b) for a, b in zip(sources, targets)]
    pick = one_hot(ids, sz)
    fill_memory(pick, mkeys, memk)
    fill_memory(pick, mvalues, memv)
    fill_bias(bias, table, buckets, sz)
    loaded[0].wait()
    for r in range(0, sz.rows, block):
        x = tokens[r : r + block, :].astype(F32)
        scale = lax.rsqrt(jnp.mean(x * x, axis=-1, keepdims=True) + EPS)
        low = (x * scale * gain1[...].reshape(1, -1)).astype(BF16)
        normed1[r : r + block, :] = low
    stores.start(normed1, normed1_hbm)
    for i, (out, out_hbm) in enumerate(((query, query_hbm), (key, key_hbm), (value, value_hbm))):
        loaded[1 + i].wait()
        for r in range(0, sz.rows, block):
            out[r : r + block, :] = nn(normed1[r : r + block, :], weights[i]).astype(BF16)
        stores.start(out, out_hbm)
    mask = head_mask(sz)

    def step(q, carry):
        length = lengths[q]
        rows = pl.ds(pl.multiple_of(q * sz.seq, sz.seq), sz.seq)
        for c in range(sz.quads):
            col = c * sz.qw
            sq = spread(query[rows, col : col + sz.qw], mask, sz)
            keys = key_block(key, memk, q, col, sz)
            values = key_block(value, memv, q, col, sz)
            probs = probabilities(keys, sq, bias[:, col : col + sz.qw], length, sz)
            full = tn(probs.astype(BF16), values)
            attended[rows, col : col + sz.qw] = gather_diag(full, sz).astype(BF16)
        return carry

    lax.fori_loop(0, sz.questions, step, 0, unroll=UNROLL_FORWARD)
    stores.start(attended, attended_hbm)
    loaded[4].wait()
    for r in range(0, sz.rows, block):
        rows = slice(r, r + block)
        h = tokens[rows, :].astype(F32) + nn(attended[rows, :], weights[3])
        hidden[rows, :] = h
        scale = lax.rsqrt(jnp.mean(h * h, axis=-1, keepdims=True) + EPS)
        normed2[rows, :] = (h * scale * gain2[...].reshape(1, -1)).astype(BF16)
        stores.start(hidden.at[pl.ds(r, block)], hidden_hbm.at[pl.ds(r, block)])
        stores.start(normed2.at[pl.ds(r, block)], normed2_hbm.at[pl.ds(r, block)])
    stores.wait()


def forward(step, sz, tokens, wq, wk, wv, wo, gain1, gain2, table, mkeys, mvalues, ids, lengths, buckets):
    n, d = sz.rows, sz.width
    low = shape((n, d), BF16)
    outs = [low, low, low, low, low, shape((n, d), F32), low]
    mem = (sz.questions * sz.pad, sz.prefix * d)
    return pl.pallas_call(
        functools.partial(forward_kernel, sz),
        in_specs=[ANY] * 5 + [VMEM] * 6 + [SMEM, VMEM],
        out_specs=[ANY] * 7,
        out_shape=outs,
        scratch_shapes=[pltpu.VMEM((n, d), BF16), pltpu.VMEM((4, d, d), BF16)]
        + [pltpu.VMEM(o.shape, o.dtype) for o in outs]
        + [
            pltpu.VMEM((sz.span, sz.heads * sz.seq), F32),
            pltpu.VMEM(mem, BF16),
            pltpu.VMEM(mem, BF16),
            pltpu.SemaphoreType.DMA((5,)),
            pltpu.SemaphoreType.DMA((5 + 2 * (n // 256),)),
        ],
        compiler_params=params(),
        cost_estimate=cost(step),
        name="forward",
    )(tokens, wq, wk, wv, wo, gain1, gain2, table, mkeys, mvalues, ids, lengths, buckets)


def unit_kernel(olds, normed2, cot, wi, wo, *refs):
    act, d_inner = refs[olds:]
    v = nn(normed2[...], wi[...])
    d_act = nt(cot[...], wo[...])
    sq = v * v
    t = jnp.tanh(v * (GELU_C + (GELU_C * GELU_A) * sq))
    half = 0.5 + 0.5 * t
    act[...] = (v * half).astype(BF16)
    slope = half + (0.5 * v) * (1.0 - t * t) * (GELU_C + (3.0 * GELU_C * GELU_A) * sq)
    d_inner[...] = (d_act * slope).astype(BF16)


def units(step, normed2, cot, wi, wo, quarter, olds=()):
    n, d = normed2.shape
    rows = pl.BlockSpec((UNIT_ROWS, d), lambda j: (j, 0))
    cols = pl.BlockSpec((UNIT_ROWS, d), lambda j: (j, quarter))
    wide = shape((n, wi.shape[1]), BF16)
    return pl.pallas_call(
        functools.partial(unit_kernel, len(olds)),
        grid=(n // UNIT_ROWS,),
        in_specs=[
            rows,
            rows,
            pl.BlockSpec((d, d), lambda j: (0, quarter)),
            pl.BlockSpec((d, d), lambda j: (quarter, 0)),
        ]
        + [ANY] * len(olds),
        out_specs=[cols, cols],
        out_shape=[wide, wide],
        input_output_aliases={4 + i: i for i in range(len(olds))},
        compiler_params=params(),
        cost_estimate=cost(step),
        name="units",
    )(normed2, cot, wi, wo, *olds)


def weight_kernel(quarter, extra, core, normed2_hbm, cot_hbm, act_hbm, d_inner_hbm, *refs):
    refs = list(refs)
    grad_out_hbm = refs.pop(0) if extra else None
    keep_hbm, send0_hbm, send1_hbm, normed2, cot, act, d_inner, keep, send, in_sems, out_sems = refs
    d = normed2.shape[1]
    h = d // 2
    cols = pl.ds(quarter * d, d)
    loads = Copies(in_sems)
    inner = [loads.start(normed2_hbm, normed2), loads.start(d_inner_hbm.at[:, cols], d_inner)]
    outer = [loads.start(act_hbm.at[:, cols], act), loads.start(cot_hbm, cot)]
    more = []
    if extra:
        for at, target in ((core[0], keep), (1 - core[0], send)):
            row = pl.multiple_of(at * h + quarter % 2 * extra, 8)
            more.append(loads.start(grad_out_hbm.at[pl.ds(row, extra)], target.at[pl.ds(d, extra)]))

    def write(first, second):
        stores = Copies(out_sems)
        for (ready, left, right), out in ((first, send), (second, keep)):
            for copy in ready:
                copy.wait()
            for i in (0, 1):
                half = slice(i * h, i * h + h)
                out[half, :] = tn(left[:, half], right[...])
            if out is send:
                for copy in more:
                    copy.wait()
                n = send0_hbm.shape[0]
                stores.start(send.at[pl.ds(0, n)], send0_hbm)
                stores.start(send.at[pl.ds(n, n)], send1_hbm)
        stores.start(keep, keep_hbm)
        stores.wait()

    @pl.when(core[0] == 0)
    def _():
        write((inner, normed2, d_inner), (outer, act, cot))

    @pl.when(core[0] != 0)
    def _():
        write((outer, act, cot), (inner, normed2, d_inner))


def weights(step, core, normed2, cot, act, d_inner, quarter, grad_out=None):
    n, d = normed2.shape
    extra = 0 if grad_out is None else d // 4
    rows = d + extra
    operands = (normed2, cot, act, d_inner) + (() if grad_out is None else (grad_out,))
    return pl.pallas_call(
        functools.partial(weight_kernel, quarter, extra),
        in_specs=[SMEM] + [ANY] * len(operands),
        out_specs=[ANY] * 3,
        out_shape=[shape((rows, d), F32)] + [shape((rows // 2, d), F32)] * 2,
        scratch_shapes=[pltpu.VMEM((n, d), BF16)] * 4
        + [pltpu.VMEM((rows, d), F32)] * 2
        + [pltpu.SemaphoreType.DMA((6,)), pltpu.SemaphoreType.DMA((3,))],
        compiler_params=params(),
        cost_estimate=cost(step),
        name="weights",
    )(core, *operands)


def mid_kernel(
    steps, d_in, wi, hidden_hbm, cot_hbm, gain2, attended_hbm, wo_hbm,
    d_hidden_hbm, d_attended_hbm, grad_out_hbm, grad_gain,
    total, hidden, cot, attended, wo, d_hidden, d_attended, grad_out, in_sems, out_sems,
):
    j = pl.program_id(0)
    block = 256
    n = hidden.shape[0]
    loads = ((hidden_hbm, hidden), (cot_hbm, cot), (wo_hbm, wo), (attended_hbm, attended))

    def load(i):
        return pltpu.make_async_copy(*loads[i], in_sems.at[i])

    @pl.when(j == 0)
    def _():
        for i in range(4):
            load(i).start()
        total[...] = nt(d_in[...], wi[...])

    @pl.when(j > 0)
    def _():
        total[...] += nt(d_in[...], wi[...])

    @pl.when(j == steps - 1)
    def _():
        stores = Copies(out_sems)
        for i in range(4):
            load(i).wait()
        acc = jnp.zeros((1, hidden.shape[1]), F32)
        for r in range(0, n, block):
            rows = slice(r, r + block)
            h = hidden[rows, :]
            scale = lax.rsqrt(jnp.mean(h * h, axis=-1, keepdims=True) + EPS)
            base = h * scale
            d_normed = total[rows, :]
            scaled = d_normed * gain2[...].reshape(1, -1)
            acc = acc + jnp.sum(d_normed * base, axis=0, keepdims=True)
            back = scale * (scaled - base * jnp.mean(scaled * base, axis=-1, keepdims=True))
            d_h = cot[rows, :].astype(F32) + back
            d_hidden[rows, :] = d_h
            low = d_h.astype(BF16)
            cot[rows, :] = low
            d_attended[rows, :] = nt(low, wo[...]).astype(BF16)
            where = pl.ds(r, block)
            stores.start(d_hidden.at[where], d_hidden_hbm.at[where])
            stores.start(d_attended.at[where], d_attended_hbm.at[where])
        grad_gain[...] = acc
        half = grad_out.shape[0] // 2
        for i in (0, 1):
            grad_out[i * half : (i + 1) * half, :] = tn(attended[:, i * half : (i + 1) * half], cot[...])
            where = pl.ds(i * half, half)
            stores.start(grad_out.at[where], grad_out_hbm.at[where])
        stores.wait()


def mid(step, d_in, wi, hidden, cot, gain2, attended, wo):
    n, d = hidden.shape
    steps = d_in.shape[1] // d
    return pl.pallas_call(
        functools.partial(mid_kernel, steps),
        grid=(steps,),
        in_specs=[
            pl.BlockSpec((n, d), lambda j: (0, j)),
            pl.BlockSpec((d, d), lambda j: (0, j)),
            ANY,
            ANY,
            pl.BlockSpec((d,), lambda j: (0,)),
            ANY,
            ANY,
        ],
        out_specs=[ANY, ANY, ANY, pl.BlockSpec((1, d), lambda j: (0, 0))],
        out_shape=[shape((n, d), F32), shape((n, d), BF16), shape((d, d), F32), shape((1, d), F32)],
        scratch_shapes=[
            pltpu.VMEM((n, d), F32),
            pltpu.VMEM((n, d), F32),
            pltpu.VMEM((n, d), BF16),
            pltpu.VMEM((n, d), BF16),
            pltpu.VMEM((d, d), BF16),
            pltpu.VMEM((n, d), F32),
            pltpu.VMEM((n, d), BF16),
            pltpu.VMEM((d, d), F32),
            pltpu.SemaphoreType.DMA((4,)),
            pltpu.SemaphoreType.DMA((2 * (n // 256) + 2,)),
        ],
        compiler_params=params(),
        cost_estimate=cost(step),
        name="mid",
    )(d_in, wi, hidden, cot, gain2, attended, wo)


def back_kernel(
    sz,
    my_core, query_hbm, key_hbm, value_hbm, d_att_hbm, normed1_hbm, mkeys, mvalues, ids, lengths, buckets,
    table, wq_hbm, wk_hbm, wv_hbm, gain1, grad_gain2,
    d_query_hbm, d_key_hbm, d_value_hbm, keep0_hbm, keep1_hbm, send00_hbm, send01_hbm, send10_hbm, send11_hbm,
    query, key, value, d_att, normed1, weights, d_query, d_key, d_value, shares,
    bias, memk, memv, d_memk, d_memv, d_bias, sums, in_sems, out_sems,
):
    d = sz.width
    h = d // 2
    loads, stores = Copies(in_sems), Copies(out_sems)
    early = [
        loads.start(a, b)
        for a, b in ((query_hbm, query), (key_hbm, key), (value_hbm, value), (d_att_hbm, d_att))
    ]
    late = [loads.start(normed1_hbm, normed1)]
    late += [loads.start(w, weights.at[i]) for i, w in enumerate((wq_hbm, wk_hbm, wv_hbm))]
    pick = one_hot(ids, sz)
    fill_memory(pick, mkeys, memk)
    fill_memory(pick, mvalues, memv)
    fill_bias(bias, table, buckets, sz)
    d_bias[...] = jnp.zeros_like(d_bias)
    mask = head_mask(sz)
    for copy in early:
        copy.wait()

    def step(q, carry):
        length = lengths[q]
        rows = pl.ds(pl.multiple_of(q * sz.seq, sz.seq), sz.seq)
        mrows = pl.ds(pl.multiple_of(q * sz.pad, sz.pad), sz.pad)
        for c in range(sz.quads):
            col = c * sz.qw
            cols = slice(col, col + sz.qw)
            sq = spread(query[rows, cols], mask, sz)
            so = spread(d_att[rows, cols], mask, sz)
            keys = key_block(key, memk, q, col, sz)
            values = key_block(value, memv, q, col, sz)
            probs = probabilities(keys, sq, bias[:, cols], length, sz)
            d_probs = nt(values, so)
            d_val = nn(probs.astype(BF16), so)
            inner = jnp.sum(probs * d_probs, axis=0, keepdims=True)
            d_scores = (probs * (d_probs - inner)).astype(BF16)
            d_bias[:, cols] += d_scores[0 : sz.seq, :].astype(F32)
            d_query[rows, cols] = gather_diag(tn(d_scores, keys), sz).astype(BF16)
            d_ky = nn(d_scores, sq)
            d_key[rows, cols] = d_ky[0 : sz.seq, :].astype(BF16)
            d_value[rows, cols] = d_val[0 : sz.seq, :].astype(BF16)
            for p in range(sz.prefix):
                part = slice(sz.seq + p * sz.pad, sz.seq + (p + 1) * sz.pad)
                to = slice(p * d + col, p * d + col + sz.qw)
                d_memk[mrows, to] = d_ky[part, :]
                d_memv[mrows, to] = d_val[part, :]
        return carry

    lax.fori_loop(0, sz.questions, step, 0, unroll=UNROLL_BACK)
    for a, b in ((d_query, d_query_hbm), (d_key, d_key_hbm), (d_value, d_value_hbm)):
        stores.start(a, b)
    for copy in late:
        copy.wait()

    mine, other = my_core[0], 1 - my_core[0]

    def store(start, keep, halves):
        stores.start(shares.at[mine, pl.ds(start, keep.shape[0])], keep)
        for half in halves:
            stores.start(shares.at[other, pl.ds(start, half.shape[0])], half)
            start += half.shape[0]

    def table_grad(full):
        high = full[...].astype(BF16)
        rest = (full[...] - high.astype(F32)).astype(BF16)
        return tn(pick, high) + tn(pick, rest)

    shares[0, 0:d, :] = tn(normed1[...], d_query[...])
    shares[1, 0:d, :] = tn(normed1[...], d_key[...])
    store(0, keep0_hbm, (send00_hbm, send01_hbm))
    for core, mem in ((0, d_memk), (1, d_memv)):
        shares[core, d : d + h, :] = tn(normed1[:, core * h : core * h + h], d_value[...])
        grads = table_grad(mem)
        for p in range(sz.prefix):
            rows = slice(d + h + p * sz.entries, d + h + (p + 1) * sz.entries)
            shares[core, rows, :] = grads[:, p * d : (p + 1) * d]

    bt = bucket_lanes(buckets, sz)
    for pair in range(sz.heads // 2):
        cols = slice(pair * 2 * sz.seq, (pair + 1) * 2 * sz.seq)
        part = d_bias[:, cols]
        for b in range(sz.buckets):
            sums[b : b + 1, cols] = jnp.sum(jnp.where(bt == float(b), part, 0.0), axis=0, keepdims=True)
    width = sz.heads * sz.seq
    head_in = lax.broadcasted_iota(jnp.int32, (width, 128), 0) // sz.seq
    head_out = lax.broadcasted_iota(jnp.int32, (width, 128), 1)
    by_head = jnp.dot(
        sums[...], jnp.where(head_in == head_out, 1.0, 0.0),
        precision=lax.Precision.HIGHEST, preferred_element_type=F32,
    )

    terms = weights[0].astype(F32) * shares[0, 0:d, :] + weights[1].astype(F32) * shares[1, 0:d, :]
    value_grad = jnp.concatenate([shares[0, d : d + h, :], shares[1, d : d + h, :]], axis=0)
    terms = terms + weights[2].astype(F32) * value_grad
    high = terms.astype(BF16)
    rest = (terms - high.astype(F32)).astype(BF16)
    ones = jnp.ones((8, d), BF16)
    total = (nt(ones, high) + nt(ones, rest))[0:1, :]
    small = d + h + sz.prefix * sz.entries
    shares[0, small : small + SMALL, :] = jnp.zeros((SMALL, d), F32)
    shares[1, small : small + SMALL, :] = jnp.zeros((SMALL, d), F32)
    shares[0, small : small + 1, :] = total / gain1[...].reshape(1, -1)
    shares[0, small + 1 : small + 2, :] = grad_gain2[...]
    shares[0, small + 8 : small + 8 + sz.buckets, 0:128] = by_head
    store(d, keep1_hbm, (send10_hbm, send11_hbm))
    stores.wait()


def back(step, sz, core, query, key, value, d_att, normed1, mkeys, mvalues, ids, lengths, buckets, table,
         wq, wk, wv, gain1, grad_gain2):
    n, d = sz.rows, sz.width
    low = shape((n, d), BF16)
    second = d // 2 + sz.prefix * sz.entries + SMALL
    mem = (sz.questions * sz.pad, sz.prefix * d)
    return pl.pallas_call(
        functools.partial(back_kernel, sz),
        in_specs=[SMEM] + [ANY] * 5 + [VMEM] * 3 + [SMEM] + [VMEM] * 2 + [ANY] * 3 + [VMEM] * 2,
        out_specs=[ANY] * 9,
        out_shape=[
            low,
            low,
            low,
            shape((d, d), F32),
            shape((second, d), F32),
            shape((d // 2, d), F32),
            shape((d // 2, d), F32),
            shape((second // 2, d), F32),
            shape((second // 2, d), F32),
        ],
        scratch_shapes=[pltpu.VMEM((n, d), BF16)] * 5
        + [pltpu.VMEM((3, d, d), BF16)]
        + [pltpu.VMEM((n, d), BF16)] * 3
        + [
            pltpu.VMEM((2, d + second, d), F32),
            pltpu.VMEM((sz.span, sz.heads * sz.seq), F32),
            pltpu.VMEM(mem, BF16),
            pltpu.VMEM(mem, BF16),
            pltpu.VMEM(mem, F32),
            pltpu.VMEM(mem, F32),
            pltpu.VMEM((sz.seq, sz.heads * sz.seq), F32),
            pltpu.VMEM((sz.buckets, sz.heads * sz.seq), F32),
            pltpu.SemaphoreType.DMA((8,)),
            pltpu.SemaphoreType.DMA((9,)),
        ],
        compiler_params=params(),
        cost_estimate=cost(step),
        name="back",
    )(core, query, key, value, d_att, normed1, mkeys, mvalues, ids, lengths, buckets, table,
      wq, wk, wv, gain1, grad_gain2)


def last_kernel(tokens, d_hidden, gain1, d_query, d_key, d_value, wq, wk, wv, grad_tokens):
    d_normed = nt(d_query[...], wq[...])
    d_normed = d_normed + nt(d_key[...], wk[...])
    d_normed = d_normed + nt(d_value[...], wv[...])
    x = tokens[...].astype(F32)
    scale = lax.rsqrt(jnp.mean(x * x, axis=-1, keepdims=True) + EPS)
    base = x * scale
    scaled = d_normed * gain1[...].reshape(1, -1)
    back_in = scale * (scaled - base * jnp.mean(scaled * base, axis=-1, keepdims=True))
    grad_tokens[...] = (d_hidden[...] + back_in).astype(BF16)


def last(step, tokens, d_hidden, gain1, d_query, d_key, d_value, wq, wk, wv):
    n, d = tokens.shape
    rows = pl.BlockSpec((256, d), lambda j: (j, 0))
    square = pl.BlockSpec((d, d), lambda j: (0, 0))
    return pl.pallas_call(
        last_kernel,
        grid=(n // 256,),
        in_specs=[rows, rows, pl.BlockSpec((d,), lambda j: (0,))] + [rows] * 3 + [square] * 3,
        out_specs=rows,
        out_shape=shape((n, d), BF16),
        compiler_params=params(),
        cost_estimate=cost(step),
        name="last",
    )(tokens, d_hidden, gain1, d_query, d_key, d_value, wq, wk, wv)


def output_kernel(hidden, act, wo, out):
    out[...] = (hidden[...] + nn(act[...], wo[...])).astype(BF16)


def output(step, hidden, act, wo):
    n, d = hidden.shape
    units_all = act.shape[1]
    rows = pl.BlockSpec((256, d), lambda j: (j, 0))
    return pl.pallas_call(
        output_kernel,
        grid=(n // 256,),
        in_specs=[
            rows,
            pl.BlockSpec((256, units_all), lambda j: (j, 0)),
            pl.BlockSpec((units_all, d), lambda j: (0, 0)),
        ],
        out_specs=rows,
        out_shape=shape((n, d), BF16),
        compiler_params=params(),
        cost_estimate=cost(step),
        name="output",
    )(hidden, act, wo)


CORE = ("dp", 1)
LINK_Y = ("dp", 2)
LINK_X = ("grp", 1)
LINK_Z = ("dp", 4)


def swap(value, link, sizes):
    axis, stride = link
    return lax.ppermute(value, axis, [(i, i ^ stride) for i in range(sizes[axis])])


def bit_of(link):
    axis, stride = link
    return (lax.axis_index(axis) // stride) % 2


class Halves:
    def __init__(self, low, high):
        self.low, self.high = low, high


def add_split_kernel(layout, bits, *refs):
    refs = list(refs)
    outs = refs[-2 * len(layout) :]
    for i, halves in enumerate(layout):
        for out, value in ((outs[2 * i], bits[i]), (outs[2 * i + 1], 1 - bits[i])):
            one = refs.pop(0)[...]
            if halves:
                low, high = refs.pop(0), refs.pop(0)
                out[...] = one + jnp.where(value == 0, low[...], high[...])
            else:
                out[...] = one + refs.pop(0)[...]


def add_split(step, bits, parts):
    steps = 2
    in_specs, out_specs, outs, operands, layout = [], [], [], [], []
    for i, (kept, got) in enumerate(parts):
        rows, d = kept.shape
        rb = rows // 2 // steps
        block = pl.BlockSpec((rb, d), lambda j, b: (j, 0))
        layout.append(isinstance(got, Halves))
        for mine in (True, False):
            for array in (kept, got):
                if isinstance(array, Halves):
                    in_specs += [block, block]
                    operands += [array.low, array.high]
                    continue

                def index(j, b, i=i, mine=mine):
                    half = b[i] if mine else 1 - b[i]
                    return (half * steps + j, 0)

                in_specs.append(pl.BlockSpec((rb, d), index))
                operands.append(array)
            out_specs.append(block)
            outs.append(shape((rows // 2, d), F32))
    result = pl.pallas_call(
        functools.partial(add_split_kernel, layout),
        grid_spec=pltpu.PrefetchScalarGridSpec(
            num_scalar_prefetch=1, grid=(steps,), in_specs=in_specs, out_specs=out_specs
        ),
        out_shape=outs,
        compiler_params=params(),
        cost_estimate=cost(step),
        name="add_split",
    )(bits, *operands)
    return [(result[2 * i], result[2 * i + 1]) for i in range(len(parts))]


def add_pairs_kernel(a, b, c, d, out0, out1):
    out0[...] = a[...] + b[...]
    out1[...] = c[...] + d[...]


def add_pairs(step, a, b, c, d):
    return pl.pallas_call(
        add_pairs_kernel,
        in_specs=[VMEM] * 4,
        out_specs=[VMEM] * 2,
        out_shape=[shape(a.shape, F32), shape(c.shape, F32)],
        compiler_params=params(),
        cost_estimate=cost(step),
        name="add_pairs",
    )(a, b, c, d)


def z_split_kernel(bit, a, b, c, d, keep, send):
    at = 0
    for left, right in ((a, b), (c, d)):
        n = left.shape[0] // 2
        for out, half in ((keep, bit[0]), (send, 1 - bit[0])):
            rows = pl.ds(pl.multiple_of(half * n, 8), n)
            out[at : at + n, :] = left[rows, :] + right[rows, :]
        at += n


def z_split(step, bit, a, b, c, d):
    out = shape(((a.shape[0] + c.shape[0]) // 2, a.shape[1]), F32)
    return pl.pallas_call(
        z_split_kernel,
        in_specs=[SMEM] + [VMEM] * 4,
        out_specs=[VMEM] * 2,
        out_shape=[out, out],
        compiler_params=params(),
        cost_estimate=cost(step),
        name="z_split",
    )(bit, a, b, c, d)


def z_mixed_kernel(bit, a, b, c, d, whole, keep, send):
    whole[...] = a[...] + b[...]
    n = c.shape[0] // 2
    for out, half in ((keep, bit[0]), (send, 1 - bit[0])):
        rows = pl.ds(pl.multiple_of(half * n, 8), n)
        out[...] = c[rows, :] + d[rows, :]


def z_mixed(step, bit, a, b, c, d):
    half = shape((c.shape[0] // 2, c.shape[1]), F32)
    return pl.pallas_call(
        z_mixed_kernel,
        in_specs=[SMEM] + [VMEM] * 4,
        out_specs=[VMEM] * 3,
        out_shape=[shape(a.shape, F32), half, half],
        compiler_params=params(),
        cost_estimate=cost(step),
        name="z_mixed",
    )(bit, a, b, c, d)


def z_add_kernel(a, b, out):
    out[...] = a[...] + b[...]


def z_add(step, a, b):
    return pl.pallas_call(
        z_add_kernel,
        in_specs=[VMEM] * 2,
        out_specs=VMEM,
        out_shape=shape(a.shape, F32),
        compiler_params=params(),
        cost_estimate=cost(step),
        name="z_add",
    )(a, b)


def z_join_kernel(bit, own, got, *outs):
    at = 0
    for out in outs:
        n = out.shape[0] // 2
        out[pl.ds(pl.multiple_of(bit[0] * n, 8), n), :] = own[at : at + n, :]
        out[pl.ds(pl.multiple_of((1 - bit[0]) * n, 8), n), :] = got[at : at + n, :]
        at += n


def z_join(step, bit, own, got, rows):
    return pl.pallas_call(
        z_join_kernel,
        in_specs=[SMEM] + [VMEM] * 2,
        out_specs=[VMEM] * len(rows),
        out_shape=[shape((r, own.shape[1]), F32) for r in rows],
        compiler_params=params(),
        cost_estimate=cost(step),
        name="z_join",
    )(bit, own, got)


def join_kernel(bits, a, b, c, d, out0, out1, both):
    at = 0
    for first, own, got, out in ((0, a, b, out0), (1, c, d, out1)):
        n = own.shape[0]
        low = pl.multiple_of(bits[first] * n, 8)
        high = pl.multiple_of((1 - bits[first]) * n, 8)
        out[pl.ds(low, n), :] = own[...]
        out[pl.ds(high, n), :] = got[...]
        both[at : at + 2 * n, :] = out[...]
        at += 2 * n


def join(step, bits, a, b, c, d):
    wide = a.shape[1]
    rows = (2 * a.shape[0], 2 * c.shape[0])
    return pl.pallas_call(
        join_kernel,
        in_specs=[SMEM] + [VMEM] * 4,
        out_specs=[VMEM] * 3,
        out_shape=[shape((r, wide), F32) for r in rows + (sum(rows),)],
        compiler_params=params(),
        cost_estimate=cost(step),
        name="join",
    )(bits, a, b, c, d)


def rest_groups(size, low):
    return [[i for i in range(size) if i % low == r] for r in range(low)]


class Order:
    def __init__(self):
        self.done = None

    def after(self, value):
        if self.done is not None:
            value, _ = lax.optimization_barrier((value, self.done))
        return value

    def run(self, kernel, step, first, *rest):
        result = kernel(step, self.after(first), *rest)
        self.done = jax.tree.leaves(result)[0]
        return result

    def wait(self, *values):
        self.done = (self.done, values)


class Reduction:
    def __init__(self, name, order, sizes, turn_by, plan, outs):
        self.name, self.order, self.sizes, self.turn_by = name, order, sizes, turn_by
        self.plan, self.outs, self.placed = plan, outs, ()
        x_bit, y_bit = bit_of(LINK_X), bit_of(LINK_Y)
        self.xy = jnp.stack([x_bit, y_bit]).astype(jnp.int32)
        self.yx = jnp.stack([y_bit, x_bit]).astype(jnp.int32)
        self.z_bit = bit_of(LINK_Z).reshape(1).astype(jnp.int32)
        self.place_bits = jnp.stack([bit_of(CORE), x_bit, y_bit]).astype(jnp.int32)
        self.links = (LINK_X, LINK_Y)
        self.kept, self.got = [None, None], [None, None]

    def run(self, kernel, stage, first, *rest):
        return self.order.run(kernel, self.name + stage, first, *rest)

    def swap(self, value, link):
        return swap(self.order.after(value), link, self.sizes)

    def begin(self, part, keep, send):
        self.kept[part] = keep
        self.got[part] = Halves(*(self.swap(half, CORE) for half in send))

    def first(self, *which):
        def kernel(step, bits):
            return add_split(step, bits, [(self.kept[i], self.got[i]) for i in which])

        halves = self.run(kernel, "1", self.xy if which == (0, 1) else self.xy[which[0] :])
        for i, (keep, send) in zip(which, halves):
            self.kept[i], self.got[i] = keep, self.swap(send, self.links[i])

    def second(self):
        halves = self.run(add_split, "2", self.yx, list(zip(self.kept, self.got)))
        for i, (keep, send) in enumerate(halves):
            self.kept[i], self.got[i] = keep, self.swap(send, self.links[1 - i])

    def z_sum(self, values):
        groups = rest_groups(self.sizes["dp"], 4)
        groups = groups[self.turn_by :] + groups[: self.turn_by]
        values = lax.psum(values, "dp", axis_index_groups=groups)
        if self.sizes["grp"] > 2:
            values = lax.psum(values, "grp", axis_index_groups=rest_groups(self.sizes["grp"], 2))
        return list(values)

    def third(self):
        pair = self.run(add_pairs, "3", self.kept[0], self.got[0], self.kept[1], self.got[1])
        self.kept = self.z_sum(tuple(pair))

    def collect(self):
        self.order.wait(self.kept[0])

    def z_start(self, keep, send):
        self.kept, self.got = keep, self.swap(send, LINK_Z)
        self.rest = [("dp", 1 << k) for k in range(3, self.sizes["dp"].bit_length() - 1)]
        self.rest += [("grp", 1 << k) for k in range(1, self.sizes["grp"].bit_length() - 1)]

    def z_first(self):
        self.whole, self.rows = [], (self.kept[0].shape[0], self.kept[1].shape[0])
        self.z_start(*self.run(z_split, "3", self.z_bit, self.kept[0], self.got[0], self.kept[1], self.got[1]))

    def z_first_mixed(self):
        self.rows = (self.kept[1].shape[0],)
        whole, keep, send = self.run(
            z_mixed, "3", self.z_bit, self.kept[0], self.got[0], self.kept[1], self.got[1]
        )
        self.whole = self.z_sum((whole,))
        self.z_start(keep, send)

    def z_second(self):
        for link in self.rest:
            self.kept = self.run(z_add, "z1", self.kept, self.got)
            self.got = self.swap(self.kept, link)

    def z_third(self):
        self.kept = self.run(z_add, "z2", self.kept, self.got)
        self.got = self.swap(self.kept, LINK_Z)

    def z_fourth(self):
        parts = self.run(z_join, "z3", self.z_bit, self.kept, self.got, self.rows)
        self.kept = self.whole + list(parts)

    def fourth(self):
        self.got = [self.swap(self.kept[i], self.links[1 - i]) for i in (0, 1)]

    def fifth(self):
        g0, g1, both = self.run(join, "5", self.yx, self.kept[0], self.got[0], self.kept[1], self.got[1])
        self.near = (g0, g1)
        self.far = tuple(self.swap(self.near[i], self.links[i]) for i in (0, 1))
        self.both = both

    def cross_near(self):
        self.other_near = (self.swap(self.both, CORE),)

    def cross_near_apart(self):
        self.other_near = tuple(self.swap(g, CORE) for g in self.near)

    def sixth(self):
        self.far = tuple(self.order.after(v) for v in self.far)
        self.order.wait(*self.far)
        self.other_far = tuple(swap(v, CORE, self.sizes) for v in self.far)

    def place(self, flip, arrays):
        def kernel(step, bits):
            return place(step, flip, self.plan, bits, arrays, self.outs, self.placed)

        self.placed = self.run(kernel, "p", self.place_bits)

    def place_near(self):
        self.place(0, self.near + self.other_near)

    def place_far(self):
        self.place(1, self.far + self.other_far)


def place_kernel(flip, plan, n_in, n_out, n_alias, bits, *refs):
    srcs = refs[:n_in]
    outs = refs[n_in + n_alias : n_in + n_alias + n_out]
    bufs = refs[n_in + n_alias + n_out : -2]
    in_sems, out_sems = refs[-2:]
    loads = [pltpu.make_async_copy(srcs[i], bufs[i], in_sems.at[i]) for i in range(n_in)]
    for load in loads:
        load.start()
    rows0 = bufs[0].shape[0]
    pieces = [(0, 0), (1, 0), (2, 0)] + [(2, rows0) if n_in == 3 else (3, 0)]
    for core in (0, 1):
        for x_bit in (0, 1):
            for y_bit in (0, 1):
                test = (bits[0] == core) & (bits[1] == x_bit) & (bits[2] == y_bit)

                @pl.when(test)
                def _(core=core, x_bit=x_bit, y_bit=y_bit):
                    copies = []
                    for index, (buf, base) in enumerate(pieces):
                        if base == 0:
                            loads[buf].wait()
                        other_core, part = index // 2, index % 2
                        key = (part, core ^ other_core, (x_bit, y_bit)[part] ^ flip)
                        for row, rows, out, where in plan[key]:
                            copies.append(
                                pltpu.make_async_copy(
                                    bufs[buf].at[pl.ds(base + row, rows)],
                                    outs[out].at[where],
                                    out_sems.at[len(copies)],
                                )
                            )
                            copies[-1].start()
                    for copy in copies:
                        copy.wait()


def place(step, flip, plan, bits, arrays, outs, olds=()):
    n_copies = 4 * max(len(v) for v in plan.values())
    return pl.pallas_call(
        functools.partial(place_kernel, flip, plan, len(arrays), len(outs), len(olds)),
        in_specs=[SMEM] + [ANY] * (len(arrays) + len(olds)),
        out_specs=[ANY] * len(outs),
        out_shape=outs,
        input_output_aliases={1 + len(arrays) + i: i for i in range(len(olds))},
        scratch_shapes=[pltpu.VMEM(a.shape, F32) for a in arrays]
        + [pltpu.SemaphoreType.DMA((len(arrays),)), pltpu.SemaphoreType.DMA((n_copies,))],
        compiler_params=params(),
        cost_estimate=cost(step),
        name="place",
    )(bits, *arrays, *olds)


def split_plan(rows, blocks):
    h = rows // 2
    plan = []
    for half in (0, 1):
        todo = []
        for start, count, out, row, cols in blocks:
            low, high = max(start, half * h), min(start + count, (half + 1) * h)
            if low < high:
                todo.append((low - half * h, high - low, out, (pl.ds(row + low - start, high - low), cols)))
        plan.append(todo)
    return plan


def ffn_plan(first, d, extra=0):
    plan = {}
    whole = pl.ds(0, d)
    for part in (0, 1):
        at = (first + part) * d
        for core, block in ((0, (0, d, 0, at, whole)), (1, (0, d, 1, 0, pl.ds(at, d)))):
            blocks = [block]
            if extra:
                blocks.append((d, extra, 2, core * d // 2 + part * extra, whole))
            for half, todo in enumerate(split_plan(d + extra, blocks)):
                plan[(part, core, half)] = todo
    return plan


def attn_plan(d, entries, prefix):
    plan = {}
    whole = pl.ds(0, d)
    h = d // 2
    small = h + prefix * entries
    for core in (0, 1):
        blocks = [(0, h, 2, core * h, whole)]
        blocks += [(h + p * entries, entries, 3 + core, 0, pl.ds(p * d, d)) for p in range(prefix)]
        if core == 0:
            blocks.append((small, SMALL, 5, 0, whole))
        for half, todo in enumerate(split_plan(d, [(0, d, core, 0, whole)])):
            plan[(0, core, half)] = todo
        for half, todo in enumerate(split_plan(small + SMALL, blocks)):
            plan[(1, core, half)] = todo
    return plan


def body(
    sizes,
    tokens,
    cotangent,
    w_query,
    w_key,
    w_value,
    w_attn_out,
    w_inner,
    w_outer,
    gain_attn,
    gain_ffn,
    bias_table,
    mem_keys,
    mem_values,
    mem_ids,
    lengths,
    buckets,
):
    questions, top = mem_ids.shape
    n, d = tokens.shape
    sz = Sizes(n, d, questions, bias_table.shape[1], bias_table.shape[0], mem_keys.shape[0], top, mem_keys.shape[1])
    table = bias_table.T
    core = bit_of(CORE).reshape(1).astype(jnp.int32)
    order = Order()
    square = shape((d, d), F32)
    mem = shape(mem_keys.shape, F32)
    ffn_outs = [shape(w_outer.shape, F32), shape(w_inner.shape, F32)]
    attn_outs = [square, square, square, mem, mem, shape((SMALL, d), F32)]
    red = {
        "A": Reduction("A", order, sizes, 0, ffn_plan(0, d), ffn_outs),
        "B": Reduction("B", order, sizes, 1, ffn_plan(2, d, d // 4), ffn_outs + [square]),
        "C": Reduction("C", order, sizes, 2, attn_plan(d, sz.entries, sz.prefix), attn_outs),
    }
    v = {"wide": ()}

    def run_forward():
        names = ("normed1", "query", "key", "value", "attended", "hidden", "normed2")
        v.update(zip(names, order.run(
            lambda step, first, *rest: forward(step, sz, first, *rest), "fwd",
            tokens, w_query, w_key, w_value, w_attn_out, gain_attn, gain_ffn, table,
            mem_keys, mem_values, mem_ids, lengths, buckets,
        )))

    def run_units(q):
        v["wide"] = tuple(order.run(units, "e", v["normed2"], cotangent, w_inner, w_outer, q, v["wide"]))

    def run_weights(q):
        grad_out = v["grad_out"] if q >= 2 else None
        keep, *send = order.run(weights, "w", core, v["normed2"], cotangent, *v["wide"], q, grad_out)
        red["AB"[q // 2]].begin(q % 2, keep, send)

    def run_mid():
        names = ("d_hidden", "d_attended", "grad_out", "grad_gain2")
        v.update(zip(names, order.run(
            mid, "mid", v["wide"][1], w_inner, v["hidden"], cotangent, gain_ffn, v["attended"], w_attn_out
        )))

    def run_back():
        names = ("d_query", "d_key", "d_value", "keep0", "keep1", "send00", "send01", "send10", "send11")
        v.update(zip(names, order.run(
            lambda step, first, *rest: back(step, sz, first, *rest), "back",
            core, v["query"], v["key"], v["value"], v["d_attended"], v["normed1"], mem_keys, mem_values,
            mem_ids, lengths, buckets, table, w_query, w_key, w_value, gain_attn, v["grad_gain2"],
        )))

    def run_last():
        v["grad_tokens"] = order.run(
            last, "last", tokens, v["d_hidden"], gain_attn, v["d_query"], v["d_key"], v["d_value"],
            w_query, w_key, w_value,
        )

    def run_output():
        v["out"] = order.run(output, "out", v["hidden"], v["wide"][0], w_outer)

    steps = {"fwd": run_forward, "mid": run_mid, "back": run_back, "last": run_last, "out": run_output}
    for q in range(4):
        steps["e%d" % q] = functools.partial(run_units, q)
        steps["w%d" % q] = functools.partial(run_weights, q)
    for name, r in red.items():
        steps.update({
            name + "1": functools.partial(r.first, 0, 1),
            name + "10": functools.partial(r.first, 0),
            name + "11": functools.partial(r.first, 1),
            name + "2": r.second, name + "3": r.third, name + "c": r.collect,
            name + "z0": r.z_first, name + "h0": r.z_first_mixed, name + "z1": r.z_second, name + "z2": r.z_third, name + "z3": r.z_fourth,
            name + "4": r.fourth, name + "5": r.fifth, name + "6": r.sixth, name + "n": r.cross_near, name + "m": r.cross_near_apart,
            name + "pn": r.place_near, name + "pf": r.place_far,
        })
    def begin_attention(part):
        red["C"].begin(part, v["keep%d" % part], (v["send%d0" % part], v["send%d1" % part]))

    for part in (0, 1):
        steps["Cb%d" % part] = functools.partial(begin_attention, part)

    def hand_over():
        red["B"].placed = red["A"].placed

    steps["AB"] = hand_over
    for step in PLAN:
        steps[step]()
    out, grad_tokens = v["out"], v["grad_tokens"]
    grad_w_outer, grad_w_inner, go = red["B"].placed
    gq, gk, gv, gmk, gmv, small = red["C"].placed
    return (
        out,
        grad_tokens,
        gq,
        gk,
        gv,
        go,
        grad_w_inner,
        grad_w_outer,
        small[0],
        small[1],
        small[8 : 8 + sz.buckets, : sz.heads],
        gmk,
        gmv,
    )


def solution(mesh):
    split = P(("grp", "dp"), None)
    placed = (split, split) + (P(),) * 11 + (split, P(("grp", "dp")), P())
    return jax.shard_map(
        functools.partial(body, dict(mesh.shape)),
        mesh=mesh,
        in_specs=placed,
        out_specs=(split, split) + (P(),) * 11,
        check_vma=False,
    )
```
